32 devices in a mesh: sub: 8 (over z, x), blk: 4 (over y, core).
Axes of the slice: x: 2, y: 2, z: 4, core: 2. Of those that a mesh axis runs over, the one named last changes fastest.
Arguments:
- residual: float32 [8, 8, 375, 256], P('sub', 'blk'), may hold values from -6 to 6
- stiffness: bfloat16 [8, 8, 16, 375, 375], P('sub', 'blk'), may hold values from -0.078125 to 0.078125
- pattern: int32 [8, 8, 16], P('sub', 'blk'), may hold values from 0 to 7
- neumann_inv: bfloat16 [8, 8, 375, 375], P('sub', 'blk'), may hold values from -0.3125 to 0.3125
- dirichlet_inv: bfloat16 [8, 8, 375, 375], P('sub', 'blk'), may hold values from -0.3125 to 0.3125
- basis: bfloat16 [8, 8, 375, 192], P('sub', 'blk'), may hold values from -0.5 to 0.5
- node_ops: float32 [8, 3, 192, 192], P('sub'), as said below
- root_inv: float32 [192, 192], replicated, may hold values from -0.4375 to 0.4375
Outputs:
- preconditioned: float32 [8, 8, 375, 256], P('sub', 'blk')
The draws below stay inside these ranges and needn't reach their ends.
Inputs may be any that keep to these rules, and one draw needn't show every extreme that they name: node_ops[s, l] equals node_ops[t, l] whenever s // 2**l == t // 2**l: one map for each tree node, held by all of its subdomains.
All inputs are finite; a program needn't handle non-finite values.
Results may differ from the reference program's by a relative error of at most 0.004.
Values may be sent and summed in bfloat16 or wider, within the bound.
No kernel may reach another device: no remote copies, remote signals or barrier semaphores. Data moves between devices by JAX's collectives and lax.ppermute only.
A program may use at most 64 MiB of HBM per device.

```python
import jax
import jax.numpy as jnp
from jax import lax

BLOCK = 375
MODES = 192
COUPLED = 16
LOADS = 256
BLK_DEV = 2
NBLOCKS = 8
NSUBS = 8
LEVELS = 3
N_BLK = 4


def draw_node_ops(key, part):
    tables = []
    for level in range(LEVELS):
        groups = NSUBS // 2 ** level
        sub_key = jax.random.fold_in(key, level + 11)
        base = jax.random.normal(sub_key, (groups, MODES, MODES), jnp.float32)
        base = base * (2.0 * MODES) ** (-0.5)
        tables.append(jnp.repeat(base, 2 ** level, axis=0))
    return jnp.stack(tables, axis=1)


def plant(result, rng, smallest, high):
    extent = result.shape
    index_at = [jax.random.randint(jax.random.fold_in(rng, axis), (), 0, extent[axis]) for axis in range(len(extent))]
    result = result.at[tuple(index_at)].set(smallest)
    longest = extent.index(max(extent))
    index_at[longest] = (index_at[longest] + 1) % extent[longest]
    return result.at[tuple(index_at)].set(high)


def steps_of(key, shape, split, least, largest):
    gain = 1.0
    for axis_at, shards_of in split:
        steps = jax.random.uniform(jax.random.fold_in(jax.random.fold_in(key, 6), axis_at), (shards_of,), jnp.float32, least / len(split), largest / len(split))
        gain = gain * jnp.repeat(jnp.exp(steps), shape[axis_at] // shards_of).reshape((-1,) + (1,) * (len(shape) - 1 - axis_at))
    return gain


def noise(stream_key, dims, width, limit, pieces=(), dtype=jnp.bfloat16):
    loudness = steps_of(stream_key, dims, pieces, -0.22, 0.18) if pieces else 1.0
    entries = jax.random.normal(stream_key, dims, jnp.float32) * width * loudness
    return jnp.minimum(jnp.maximum(entries, -limit), limit).astype(dtype)


def setup_inputs(seed: int = 0) -> dict:
    splits = jax.random.split(jax.random.key(seed), 9)
    return {
        "residual": noise(splits[0], (NSUBS, NBLOCKS, BLOCK, LOADS), 1.0, 6.0, ((0, 8), (1, 4)), jnp.float32),
        "stiffness": noise(splits[1], (NSUBS, NBLOCKS, COUPLED, BLOCK, BLOCK), (COUPLED * BLOCK) ** -0.5, 0.078125, ((0, 8), (1, 4))),
        "pattern": plant(jax.random.randint(splits[2], (NSUBS, NBLOCKS, COUPLED), 0, NBLOCKS), jax.random.fold_in(splits[2], 1), 0, NBLOCKS - 1).astype(jnp.int32),
        "neumann_inv": noise(splits[3], (NSUBS, NBLOCKS, BLOCK, BLOCK), BLOCK ** -0.5, 0.3125, ((0, 8), (1, 4))),
        "dirichlet_inv": noise(splits[4], (NSUBS, NBLOCKS, BLOCK, BLOCK), BLOCK ** -0.5, 0.3125, ((0, 8), (1, 4))),
        "basis": noise(splits[5], (NSUBS, NBLOCKS, BLOCK, MODES), ((NBLOCKS * BLOCK * MODES) ** -0.25), 0.5, ((0, 8), (1, 4))),
        "node_ops": draw_node_ops(jax.random.fold_in(splits[8], 71), 0),
        "root_inv": noise(splits[7], (MODES, MODES), MODES ** -0.5, 0.4375, (), jnp.float32),
    }


def shared_faces():
    sub_ids = jnp.arange(NSUBS)[:, None]
    local_ids = (jnp.arange(NBLOCKS) % BLK_DEV)[None, :]
    return ((local_ids == 0) & (sub_ids > 0)) | ((local_ids == BLK_DEV - 1) & (sub_ids < NSUBS - 1))


def local_part(items):
    values, inverse, modes = items
    values = values.astype(jnp.float32)
    local_fix = jnp.einsum('jab,jbr->jar', inverse.astype(jnp.float32), values)
    coarse = jnp.einsum('jbm,jbr->mr', modes.astype(jnp.float32), values)
    return local_fix, coarse


def coarse_part(items):
    modes, coarse_fix = items
    return jnp.einsum('jbm,mr->jbr', modes.astype(jnp.float32), coarse_fix.astype(jnp.float32))


def dirichlet(items):
    values, coupling, columns, inverse = items
    picked = jnp.take(values, columns.astype(jnp.int32), axis=0).astype(jnp.float32)
    coupled = jnp.einsum('jpab,jpbr->jar', coupling.astype(jnp.float32), picked)
    coupled_bf = lax.optimization_barrier(coupled.astype(jnp.bfloat16))
    return jnp.einsum('jab,jbr->jar', inverse.astype(jnp.float32), coupled_bf.astype(jnp.float32))


def reference(residual, stiffness, pattern, neumann_inv, dirichlet_inv, basis, node_ops, root_inv):
    shared = shared_faces()
    scale = jnp.where(shared, 0.5, 1.0).astype(jnp.float32)[:, :, None, None]
    scaled_bf = lax.optimization_barrier((residual * scale).astype(jnp.bfloat16))
    local_fix, coarse = lax.map(local_part, (scaled_bf, neumann_inv, basis))
    highest = lax.Precision.HIGHEST
    sub_ids = jnp.arange(NSUBS)
    level_values = [coarse]
    current = coarse
    for level in range(LEVELS):
        own = jnp.einsum('smk,smr->skr', node_ops[:, level], current, precision=highest)
        current = own + own[sub_ids ^ (1 << level)]
        level_values.append(current)
    field = jnp.einsum('km,smr->skr', root_inv, current, precision=highest)
    for level in reversed(range(LEVELS)):
        field = jnp.einsum('smk,skr->smr', node_ops[:, level], field, precision=highest) + level_values[level]
    coarse_fix = lax.optimization_barrier(field.astype(jnp.bfloat16))
    fix_term = lax.map(coarse_part, (basis, coarse_fix))
    combined = (local_fix + fix_term) * scale
    blocks = combined.reshape(NSUBS, N_BLK, BLK_DEV, BLOCK, LOADS)
    zero_face = jnp.zeros((1, N_BLK, BLOCK, LOADS), jnp.float32)
    from_prev = jnp.concatenate([zero_face, blocks[:-1, :, BLK_DEV - 1]], axis=0)
    from_next = jnp.concatenate([blocks[1:, :, 0], zero_face], axis=0)
    first = blocks[:, :, 0] + from_prev
    last = blocks[:, :, BLK_DEV - 1] + from_next
    assembled = blocks.at[:, :, 0].set(first).at[:, :, BLK_DEV - 1].set(last)
    assembled = assembled.reshape(NSUBS, NBLOCKS, BLOCK, LOADS)
    assembled_bf = lax.optimization_barrier(assembled.astype(jnp.bfloat16))
    correction = lax.map(dirichlet, (assembled_bf, stiffness, pattern, dirichlet_inv))
    return assembled - jnp.where(shared[:, :, None, None], 0.0, correction)
```

```python
import functools

import jax
import jax.numpy as jnp
from jax import lax
from jax.experimental import pallas as pl
from jax.experimental.pallas import tpu as pltpu
from jax.sharding import PartitionSpec as P

HIGHEST = lax.Precision.HIGHEST
BF = jnp.bfloat16
F32 = jnp.float32


def route(x, subs, blks, target):
    pairs = []
    for s in range(subs):
        for b in range(blks):
            to = target(s, b)
            if to is not None and 0 <= to[0] < subs and 0 <= to[1] < blks:
                pairs.append((s * blks + b, to[0] * blks + to[1]))
    return lax.ppermute(x, ("sub", "blk"), pairs)


def dot(a, b):
    return jnp.dot(a, b, precision=HIGHEST, preferred_element_type=F32)


def tdot(a, b):
    return lax.dot_general(
        a, b, (((0,), (0,)), ((), ())), precision=HIGHEST, preferred_element_type=F32
    )


def stiffness_kernel(pattern_ref, matrix_ref, values_ref, inverse_ref, out_ref):
    total = jnp.zeros(out_ref.shape, F32)
    for k in range(matrix_ref.shape[0]):
        total += jnp.dot(
            matrix_ref[k], values_ref[pattern_ref[k]], preferred_element_type=F32
        )
    out_ref[...] = jnp.dot(
        inverse_ref[...], total.astype(BF), preferred_element_type=F32
    )


def corrected(columns, matrix, values, inverse):
    coupled, block, _ = matrix.shape
    loads = values.shape[-1]
    vmem = pl.BlockSpec(memory_space=pltpu.VMEM)
    return pl.pallas_call(
        stiffness_kernel,
        out_shape=jax.ShapeDtypeStruct((block, loads), F32),
        in_specs=[pl.BlockSpec(memory_space=pltpu.SMEM), vmem, vmem, vmem],
        out_specs=vmem,
        compiler_params=pltpu.CompilerParams(vmem_limit_bytes=32 * 1024 * 1024),
        cost_estimate=pl.CostEstimate(
            flops=2 * coupled * block * block * loads,
            bytes_accessed=2 * coupled * block * block,
            transcendentals=0,
        ),
    )(columns, matrix, values, inverse)


def shards(subs, blks, residual, stiffness, pattern, neumann_inv, dirichlet_inv, basis, node_ops, root_inv):
    here = lax.axis_index("sub")
    mine = lax.axis_index("blk")
    per = residual.shape[1]
    levels = node_ops.shape[1]
    even = here % 2 == 0
    edge = (here == 0) | (here == subs - 1)
    go = functools.partial(route, subs=subs, blks=blks)

    def lead(f):
        return lambda s, b: f(s, b) if b % 2 == 1 else None

    local_ids = jnp.arange(per)
    shared = (local_ids == 0) & (here > 0) | (local_ids == per - 1) & (here < subs - 1)
    scale = jnp.where(shared, 0.5, 1.0).astype(F32)[:, None, None]
    scaled_bf = (residual[0] * scale).astype(BF)
    modes = basis[0]

    partial = jnp.einsum("jbm,jbr->mr", modes, scaled_bf, preferred_element_type=F32)
    coarse = partial + go(partial, target=lambda s, b: (s, b ^ 1) if b % 2 == 0 else None)
    step = 2
    while step < blks:
        coarse = coarse + go(coarse.astype(BF), target=lead(lambda s, b, k=step: (s, b ^ k))).astype(F32)
        step *= 2

    local_fix = jnp.einsum("jab,jbr->jar", neumann_inv[0], scaled_bf, preferred_element_type=F32)
    local_bf = local_fix.astype(BF)

    first = jnp.concatenate([modes[0], local_bf[0]], axis=1)
    last = jnp.concatenate([modes[-1], local_bf[-1]], axis=1)
    to_sibling = jnp.where(even, last, first)
    to_far = jnp.where(even, first, last)
    far = lambda s, b: (s - 1 if s % 2 == 0 else s + 1, b)
    from_sibling = go(to_sibling, target=lambda s, b: (s ^ 1, b))
    from_far = go(to_far, target=far)

    maps = node_ops[0]
    sibling_map = go(maps[0], target=lead(lambda s, b: (s ^ 1, b)))
    top = root_inv
    for level in reversed(range(1, levels)):
        top = dot(maps[level], top)
    own_top = dot(maps[0], top)
    sibling_top = dot(sibling_map, top)
    across = lead(lambda s, b: (s + 2 if s % 2 == 0 else s - 2, b))
    far_top = go(sibling_top.astype(BF), target=across).astype(F32)

    sibling = go(coarse.astype(BF), target=lead(lambda s, b: (s ^ 1, b))).astype(F32)
    current = tdot(maps[0], coarse) + tdot(sibling_map, sibling)
    values = [coarse, current]
    for level in range(1, levels):
        own = tdot(maps[level], current)
        if level == levels - 1:
            down = current
            for below in reversed(range(1, levels - 1)):
                down = dot(maps[below], down) + values[below]
            own_rest = dot(maps[0], down) + coarse
            sibling_rest = dot(sibling_map, down) + sibling
            far_rest = go(sibling_rest.astype(BF), target=across).astype(F32)
        current = own + go(own.astype(BF), target=lead(lambda s, b, k=2**level: (s ^ k, b))).astype(F32)
        values.append(current)
    fields = jnp.stack(
        [
            dot(own_top, current) + own_rest,
            dot(sibling_top, current) + sibling_rest,
            dot(far_top, current) + far_rest,
        ]
    ).astype(BF)
    sent = go(fields, target=lambda s, b: (s, b ^ 1) if b % 2 == 1 else None)
    fields = jnp.where(mine % 2 == 1, fields, sent)

    def spread(mode_block, field):
        return jnp.dot(mode_block, field, preferred_element_type=F32)

    width = modes.shape[-1]

    def face(received, field):
        return 0.5 * (received[:, width:].astype(F32) + spread(received[:, :width], field))

    combined = [(local_fix[j] + spread(modes[j], fields[0])) * scale[j] for j in range(per)]
    sibling_face = face(from_sibling, fields[1])
    far_face = jnp.where(edge, 0.0, face(from_far, fields[2]))
    assembled = list(combined)
    assembled[0] = combined[0] + jnp.where(even, far_face, sibling_face)
    assembled[-1] = combined[-1] + jnp.where(even, sibling_face, far_face)

    wanted = lambda s: per > 2 or s in (0, subs - 1)
    gathered = jnp.stack(assembled).astype(BF)
    step = blks // 2
    while step:
        more = go(gathered, target=lambda s, b, k=step: (s, b ^ k) if wanted(s) else None)
        gathered = jnp.concatenate([gathered, more])
        step //= 2
    order = [0]
    step = blks // 2
    while step:
        order = order + [d ^ step for d in order]
        step //= 2
    place = jnp.array([order.index(d) for d in range(blks)], jnp.int32)
    columns = place[(pattern[0] // per) ^ mine] * per + pattern[0] % per

    def correction(j):
        return corrected(columns[j], stiffness[0, j], gathered, dirichlet_inv[0, j])

    def picked(x):
        return jnp.where(here == 0, x[0], x[per - 1])

    edge_fix = corrected(
        picked(columns),
        lax.dynamic_index_in_dim(stiffness[0], jnp.where(here == 0, 0, per - 1), 0, False),
        gathered,
        picked(dirichlet_inv[0]),
    )
    result = []
    for j in range(per):
        if 0 < j < per - 1:
            fix = correction(j)
        else:
            fix = jnp.where(shared[j], 0.0, edge_fix)
        result.append(assembled[j] - fix)
    return jnp.stack(result)[None]


def solution(mesh):
    placed = (
        P("sub", "blk", None, None),
        P("sub", "blk", None, None, None),
        P("sub", "blk", None),
        P("sub", "blk", None, None),
        P("sub", "blk", None, None),
        P("sub", "blk", None, None),
        P("sub", None, None, None),
        P(),
    )
    return jax.shard_map(
        functools.partial(shards, mesh.shape["sub"], mesh.shape["blk"]),
        mesh=mesh,
        in_specs=placed,
        out_specs=P("sub", "blk", None, None),
        check_vma=False,
    )
```

```python
import functools

import jax
import jax.numpy as jnp
from jax import lax
from jax.experimental import pallas as pl
from jax.experimental.pallas import tpu as pltpu
from jax.sharding import PartitionSpec as P

HIGHEST = lax.Precision.HIGHEST
BF = jnp.bfloat16
F32 = jnp.float32
VMEM = pl.BlockSpec(memory_space=pltpu.VMEM)
SMEM = pl.BlockSpec(memory_space=pltpu.SMEM)


def route(x, subs, blks, target):
    pairs = []
    for s in range(subs):
        for b in range(blks):
            to = target(s, b)
            if to is not None and 0 <= to[0] < subs:
                pairs.append((s * blks + b, to[0] * blks + to[1]))
    return lax.ppermute(x, ("sub", "blk"), pairs)


def dot(a, b):
    return jnp.dot(a, b, precision=HIGHEST, preferred_element_type=F32)


def tdot(a, b):
    return lax.dot_general(
        a, b, (((0,), (0,)), ((), ())), precision=HIGHEST, preferred_element_type=F32
    )


def bdot(a, b):
    return jnp.dot(a, b, preferred_element_type=F32)


def call(kernel, outs, specs, flops, moved):
    return pl.pallas_call(
        kernel,
        out_shape=outs,
        in_specs=specs,
        out_specs=jax.tree.map(lambda _: VMEM, outs),
        compiler_params=pltpu.CompilerParams(vmem_limit_bytes=32 * 1024 * 1024),
        cost_estimate=pl.CostEstimate(flops=flops, bytes_accessed=moved, transcendentals=0),
    )


def face_kernel(edge_ref, fields_ref, near_ref, far_ref, near_in_ref, far_in_ref, own_ref, near_out, far_out, near_bf, mine_bf):
    loads = own_ref.shape[-1]
    field = fields_ref[0]
    scale = jnp.where(edge_ref[0] > 0, 1.0, 0.5).astype(F32)
    far = (own_ref[1] + bdot(far_ref[:, loads:], field)) * scale
    far_out[...] = far
    mine_bf[0] = far.astype(BF)
    own = own_ref[0] + bdot(near_ref[:, loads:], field)
    other = near_in_ref[:, :loads].astype(F32) + bdot(near_in_ref[:, loads:], fields_ref[1])
    near = 0.5 * own + 0.5 * other
    near_out[...] = near
    near_bf[...] = near.astype(BF)
    mine_bf[1] = near.astype(BF)
    for i in range(far_in_ref.shape[0]):
        block = far_in_ref[i, :, :loads].astype(F32) + bdot(far_in_ref[i, :, loads:], field)
        mine_bf[2 + i] = (block * scale).astype(BF)


def finish_kernel(slots_ref, flags_ref, matrix_ref, inverse_ref, mine_ref, core_ref, late_ref, late_core_ref, far_ref, far_in_ref, near_ref, out_ref, values_ref, total_ref):
    count = mine_ref.shape[0]
    more = late_ref.shape[0]
    is_edge = flags_ref[0] > 0

    @pl.when(is_edge)
    def _():
        values_ref[:count] = mine_ref[...]
        values_ref[count : 2 * count] = core_ref[...]
        values_ref[2 * count : 2 * count + more] = late_ref[...]
        values_ref[2 * count + more :] = late_core_ref[...]
        total = jnp.zeros(total_ref.shape, F32)
        for k in range(matrix_ref.shape[0]):
            total += bdot(matrix_ref[k], values_ref[slots_ref[k]])
        total_ref[...] = far_ref[...] - bdot(inverse_ref[...], total.astype(BF))

    @pl.when(jnp.logical_not(is_edge))
    def _():
        total_ref[...] = far_ref[...] + far_in_ref[...].astype(F32)

    is_even = flags_ref[1] > 0
    far = total_ref[...]
    near = near_ref[...]
    out_ref[0] = jnp.where(is_even, far, near)
    out_ref[1] = jnp.where(is_even, near, far)


def after(x, *others):
    return lax.optimization_barrier((x,) + others)[0]


def shards(subs, blks, residual, stiffness, pattern, neumann_inv, dirichlet_inv, basis, node_ops, root_inv):
    here = lax.axis_index("sub")
    mine = lax.axis_index("blk")
    _, per, block, loads = residual.shape
    width = basis.shape[-1]
    levels = node_ops.shape[1]
    assert per == 2 and levels > 2
    even = here % 2 == 0
    edge = (here == 0) | (here == subs - 1)
    upper = mine % 2 == 1
    go = functools.partial(route, subs=subs, blks=blks)
    others = range(2, blks, 2)

    def swap(x, sub=0, blk=0):
        return go(x, target=lambda s, b: (s ^ sub, b ^ blk))

    local_ids = jnp.arange(per)
    shared = (local_ids == 0) & (here > 0) | (local_ids == per - 1) & (here < subs - 1)
    scale = jnp.where(shared, 0.5, 1.0).astype(F32)[:, None, None]
    scaled_bf = (residual[0] * scale).astype(BF)
    modes = basis[0]
    maps = node_ops[0]

    partial = jnp.einsum("jbm,jbr->mr", modes, scaled_bf, preferred_element_type=F32)
    halves = partial[:, : loads // 2], partial[:, loads // 2 :]
    half = jnp.where(upper, halves[1], halves[0])
    half = half + swap(jnp.where(upper, halves[0], halves[1]), blk=1)
    half_bf = half.astype(BF)

    sibling_map = swap(maps[0], sub=1)

    local_fix = jnp.einsum("jab,jbr->jar", neumann_inv[0], scaled_bf, preferred_element_type=F32)
    local_bf = local_fix.astype(BF)

    coarse = half
    for d in others:
        coarse = coarse + swap(half_bf, blk=d).astype(F32)
    sibling = swap(half_bf, sub=1).astype(F32)
    for d in others:
        sibling = sibling + swap(half_bf, sub=1, blk=d).astype(F32)

    current = tdot(maps[0], coarse) + tdot(sibling_map, sibling)
    own = tdot(maps[1], current)
    own_bf = own.astype(BF)
    quad = own + swap(own_bf, sub=2).astype(F32)
    other_map = swap(maps[2], sub=4)
    other_quad = swap(own_bf, sub=4).astype(F32) + swap(own_bf, sub=6).astype(F32)
    payload = [jnp.concatenate([local_bf[j], modes[j]], axis=1) for j in range(per)]
    to_sibling = jnp.where(even, payload[1], payload[0])
    to_far = jnp.where(even, payload[0], payload[1])
    to_sibling, to_far = after(to_sibling, coarse, sibling), after(to_far, coarse, sibling)
    from_sibling = swap(to_sibling, sub=1)
    from_others = jnp.stack([swap(to_far, blk=d) for d in others])
    values = [coarse, current, quad]
    current = tdot(maps[2], quad) + tdot(other_map, other_quad)
    for level in range(3, levels):
        values.append(current)
        own = tdot(maps[level], current)
        current = own + swap(own.astype(BF), sub=2**level).astype(F32)
    field = dot(root_inv, current)
    for level in reversed(range(1, levels)):
        field = dot(maps[level], field) + values[level]
    fields = jnp.stack([dot(maps[0], field) + coarse, dot(sibling_map, field) + sibling]).astype(BF)
    across = swap(fields, blk=1)
    fields = jnp.concatenate(
        [jnp.where(upper, across, fields), jnp.where(upper, fields, across)], axis=2
    )

    shape = jax.ShapeDtypeStruct
    count = 2 + len(others)
    near, far, near_bf, mine_bf = call(
        face_kernel,
        (
            shape((block, loads), F32),
            shape((block, loads), F32),
            shape((block, loads), BF),
            shape((count, block, loads), BF),
        ),
        [SMEM] + [VMEM] * 6,
        2 * (count + 1) * block * width * loads,
        count * block * loads * 8,
    )(
        edge.astype(jnp.int32)[None],
        fields,
        to_sibling,
        to_far,
        from_sibling,
        from_others,
        jnp.where(even, local_fix[::-1], local_fix),
    )

    late = jnp.stack([swap(near_bf, blk=d) for d in others])
    core = swap(mine_bf, blk=1)
    far_in = go(
        mine_bf[0],
        target=lambda s, b: (s - 1 if s % 2 == 0 else s + 1, b),
    )
    late_core = swap(late, blk=1)
    slot = {(0, 0): 0, (0, 1): 1, (1, 0): count, (1, 1): count + 1}
    for i, d in enumerate(others):
        slot[d, 0], slot[d ^ 1, 0] = 2 + i, count + 2 + i
        slot[d, 1], slot[d ^ 1, 1] = 2 * count + i, 2 * count + len(others) + i
    table = jnp.array([[slot[d, k] for k in range(2)] for d in range(blks)], jnp.int32)
    far_id = jnp.where(even, 0, per - 1)
    columns = pattern[0, far_id]
    slots = table[(columns // per) ^ mine, (columns % per != far_id).astype(jnp.int32)]
    result = pl.pallas_call(
        finish_kernel,
        out_shape=shape((per, block, loads), F32),
        in_specs=[SMEM, SMEM] + [VMEM] * 9,
        out_specs=VMEM,
        scratch_shapes=[
            pltpu.VMEM((blks * per, block, loads), BF),
            pltpu.VMEM((block, loads), F32),
        ],
        compiler_params=pltpu.CompilerParams(vmem_limit_bytes=32 * 1024 * 1024),
        cost_estimate=pl.CostEstimate(
            flops=2 * pattern.shape[-1] * block * block * loads,
            bytes_accessed=2 * pattern.shape[-1] * block * block,
            transcendentals=0,
        ),
    )(
        slots,
        jnp.stack([edge, even]).astype(jnp.int32),
        lax.dynamic_index_in_dim(stiffness[0], far_id, 0, False),
        lax.dynamic_index_in_dim(dirichlet_inv[0], far_id, 0, False),
        mine_bf,
        core,
        late,
        late_core,
        far,
        far_in,
        near,
    )
    return result[None]


def solution(mesh):
    placed = (
        P("sub", "blk", None, None),
        P("sub", "blk", None, None, None),
        P("sub", "blk", None),
        P("sub", "blk", None, None),
        P("sub", "blk", None, None),
        P("sub", "blk", None, None),
        P("sub", None, None, None),
        P(),
    )
    return jax.shard_map(
        functools.partial(shards, mesh.shape["sub"], mesh.shape["blk"]),
        mesh=mesh,
        in_specs=placed,
        out_specs=P("sub", "blk", None, None),
        check_vma=False,
    )
```

```python
import functools

import jax
import jax.numpy as jnp
from jax import lax
from jax.experimental import pallas as pl
from jax.experimental.pallas import tpu as pltpu
from jax.sharding import PartitionSpec as P

BF = jnp.bfloat16
F32 = jnp.float32
VMEM = pl.BlockSpec(memory_space=pltpu.VMEM)
SMEM = pl.BlockSpec(memory_space=pltpu.SMEM)
HBM = pl.BlockSpec(memory_space=pltpu.HBM)


def route(x, subs, blks, target):
    pairs = []
    for s in range(subs):
        for b in range(blks):
            to = target(s, b)
            if to is not None and 0 <= to[0] < subs:
                pairs.append((s * blks + b, to[0] * blks + to[1]))
    return lax.ppermute(x, ("sub", "blk"), pairs)


def product(a, b, dims):
    a_high, b_high = a.astype(BF), b.astype(BF)
    a_low, b_low = (a - a_high.astype(F32)).astype(BF), (b - b_high.astype(F32)).astype(BF)
    part = functools.partial(
        lax.dot_general, dimension_numbers=(dims, ((), ())), preferred_element_type=F32
    )
    return part(a_high, b_high) + (part(a_high, b_low) + part(a_low, b_high))


def dot(a, b):
    return product(a, b, ((1,), (0,)))


def tdot(a, b):
    return product(a, b, ((0,), (0,)))


def bdot(a, b):
    return jnp.dot(a, b, preferred_element_type=F32)


def call(kernel, outs, specs, flops, moved, scratch=(), limit=16):
    return pl.pallas_call(
        kernel,
        out_shape=outs,
        in_specs=specs,
        out_specs=jax.tree.map(lambda _: VMEM, outs),
        scratch_shapes=scratch,
        compiler_params=pltpu.CompilerParams(vmem_limit_bytes=limit * 2**20),
        cost_estimate=pl.CostEstimate(flops=flops, bytes_accessed=moved, transcendentals=0),
    )


def rows_of(ref, j, part):
    rows, parts, blocks, lanes = ref.shape
    flat = ref.reshape(rows * parts * blocks, lanes)
    return flat, pl.ds(part * blocks + j, rows, stride=parts * blocks)


def start_kernel(flags_ref, residual_hbm, *refs):
    given = (len(refs) - 5) // 2
    sources, loaded = refs[:given], refs[given : 2 * given]
    scaled_ref, keep_ref, send_ref, residual_ref, sems = refs[2 * given :]
    modes_ref, maps_ref = loaded[:2]
    copies = [
        pltpu.make_async_copy(source, target, sems.at[i])
        for i, (source, target) in enumerate(zip((residual_hbm,) + sources, (residual_ref,) + loaded))
    ]
    for copy in copies:
        copy.start()
    is_even, is_edge, is_upper = (flags_ref[i] > 0 for i in range(3))
    per, _, loads = scaled_ref.shape
    lanes = residual_ref.shape[-1]
    total = jnp.zeros((modes_ref.shape[1], loads), F32)
    copies[0].wait()
    copies[1].wait()
    for j in range(per):
        is_far = is_even if j == 0 else jnp.logical_not(is_even)
        scale = jnp.where(is_edge & is_far, 1.0, 0.5).astype(F32)
        for part in range(loads // lanes):
            flat, rows = rows_of(residual_ref, j, part)
            scaled_ref[j, :, part * lanes : (part + 1) * lanes] = (flat[rows, :] * scale).astype(BF)
        total += bdot(modes_ref[j], scaled_ref[j])
    copies[2].wait()
    mapped = tdot(maps_ref[0], total)
    for i, values in enumerate((total, mapped)):
        low, high = values[:, : loads // 2], values[:, loads // 2 :]
        keep_ref[i] = jnp.where(is_upper, high, low)
        send_ref[i] = jnp.where(is_upper, low, high)
    for copy in copies[3:]:
        copy.wait()


def local_kernel(flags_ref, scaled_ref, inverse_hbm, modes_ref, near_ref, far_ref, near_out, far_out, inverse_ref, sem):
    copy = pltpu.make_async_copy(inverse_hbm, inverse_ref, sem)
    copy.start()
    loads = scaled_ref.shape[-1]
    is_even = flags_ref[0] > 0
    low_modes, high_modes = (modes_ref[j].T for j in range(2))
    near_out[:, loads:] = jnp.where(is_even, high_modes, low_modes)
    far_out[:, loads:] = jnp.where(is_even, low_modes, high_modes)
    copy.wait()
    inverse = inverse_ref[...]
    low, high = (bdot(inverse[:, j, :], scaled_ref[j]) for j in range(2))
    near, far = jnp.where(is_even, high, low), jnp.where(is_even, low, high)
    near_ref[...] = near
    far_ref[...] = far
    near_out[:, :loads] = near.astype(BF)
    far_out[:, :loads] = far.astype(BF)


def pair_kernel(keep_ref, got_ref, same_ref, cross_ref, map_ref, coarse_ref, pair_ref, own_ref, sent_ref, pack_ref):
    coarse = keep_ref[0] + got_ref[0]
    for i in range(same_ref.shape[0]):
        coarse += same_ref[i].astype(F32)
    pair = tdot(map_ref[0], coarse)
    for i in range(cross_ref.shape[0]):
        pair += cross_ref[i].astype(F32)
    own = tdot(map_ref[1], pair)
    coarse_ref[...] = coarse
    pair_ref[...] = pair
    own_ref[...] = own
    sent_ref[...] = own.astype(BF)
    columns = coarse.shape[-1]
    pack_ref[:, :columns] = coarse.astype(BF)
    pack_ref[:, columns:] = map_ref[0].astype(BF)


def level_kernel(level, own_ref, got_ref, map_ref, value_ref, next_ref, sent_ref):
    value = own_ref[...] + got_ref[...].astype(F32)
    value_ref[...] = value
    following = tdot(map_ref[level], value)
    next_ref[...] = following
    sent_ref[...] = following.astype(BF)


def down_kernel(own_ref, got_ref, pack_ref, map_ref, root_ref, coarse_ref, *refs):
    values, fields_ref = refs[:-1], refs[-1]
    field = dot(root_ref[...], own_ref[...] + got_ref[...].astype(F32))
    for level in reversed(range(1, map_ref.shape[0])):
        field = dot(map_ref[level], field) + values[level - 1][...]
    fields_ref[0] = (dot(map_ref[0], field) + coarse_ref[...]).astype(BF)
    columns = field.shape[-1]
    sibling_map = pack_ref[:, columns:].astype(F32)
    fields_ref[1] = (dot(sibling_map, field) + pack_ref[:, :columns].astype(F32)).astype(BF)


def face_kernel(flags_ref, fields_ref, near_ref, far_ref, near_in_ref, far_in_ref, near_fix_ref, far_fix_ref, near_out, far_out, near_bf, mine_bf):
    loads = near_fix_ref.shape[-1]
    field = fields_ref[0]
    scale = jnp.where(flags_ref[1] > 0, 1.0, 0.5).astype(F32)
    far = (far_fix_ref[...] + bdot(far_ref[:, loads:], field)) * scale
    far_out[...] = far
    mine_bf[0] = far.astype(BF)
    own = near_fix_ref[...] + bdot(near_ref[:, loads:], field)
    other = near_in_ref[:, :loads].astype(F32) + bdot(near_in_ref[:, loads:], fields_ref[1])
    near = 0.5 * own + 0.5 * other
    near_out[...] = near
    near_bf[...] = near.astype(BF)
    mine_bf[1] = near.astype(BF)
    for i in range(far_in_ref.shape[0]):
        block = far_in_ref[i, :, :loads].astype(F32) + bdot(far_in_ref[i, :, loads:], field)
        mine_bf[2 + i] = (block * scale).astype(BF)


def gather_products(slots_ref, first, matrix_ref, sources, values_ref, list_ref, total):
    start = 0
    for source in sources:
        values_ref[start : start + source.shape[0]] = source[...]
        start += source.shape[0]
    values_ref[start] = jnp.zeros(values_ref.shape[1:], BF)
    number = matrix_ref.shape[0]
    width = 4
    for i in range(number):
        list_ref[0, i], list_ref[1, i] = 0, start

    def note(k, found):
        slot = slots_ref[k] - first
        is_here = (slot >= 0) & (slot < start)

        @pl.when(is_here)
        def _():
            list_ref[0, found], list_ref[1, found] = k, slot

        return found + is_here.astype(jnp.int32)

    found = lax.fori_loop(0, number, note, 0)

    def add(step, carry):
        products = None
        for i in range(width):
            at = step * width + i
            one = bdot(matrix_ref[list_ref[0, at]], values_ref[list_ref[1, at]])
            products = one if products is None else products + one
        total[...] += products
        return carry

    lax.fori_loop(0, (found + width - 1) // width, add, 0)


def couple_kernel(slots_ref, flags_ref, matrix_ref, inverse_ref, mine_ref, core_ref, total_ref, picked_ref, values_ref, list_ref):
    @pl.when(flags_ref[1] > 0)
    def _():
        inverse = inverse_ref[...]
        picked_ref[...] = jnp.where(flags_ref[0] > 0, inverse[:, 0, :], inverse[:, 1, :])
        total_ref[...] = jnp.zeros(total_ref.shape, F32)
        gather_products(slots_ref, 0, matrix_ref, (mine_ref, core_ref), values_ref, list_ref, total_ref)


def finish_kernel(slots_ref, flags_ref, first, matrix_ref, picked_ref, total_ref, late_ref, late_core_ref, far_ref, far_in_ref, near_ref, out_ref, sum_ref, values_ref, list_ref):
    is_even = flags_ref[0] > 0
    is_edge = flags_ref[1] > 0

    @pl.when(is_edge)
    def _():
        sum_ref[...] = total_ref[...]
        gather_products(slots_ref, first, matrix_ref, (late_ref, late_core_ref), values_ref, list_ref, sum_ref)
        sum_ref[...] = far_ref[...] - bdot(picked_ref[...], sum_ref[...].astype(BF))

    @pl.when(jnp.logical_not(is_edge))
    def _():
        sum_ref[...] = far_ref[...] + far_in_ref[...].astype(F32)

    _, parts, _, lanes = out_ref.shape
    for part in range(parts):
        columns = slice(part * lanes, (part + 1) * lanes)
        far, near = sum_ref[:, columns], near_ref[:, columns]
        for j, values in enumerate((jnp.where(is_even, far, near), jnp.where(is_even, near, far))):
            flat, rows = rows_of(out_ref, j, part)
            flat[rows, :] = values


def after(x, *others):
    return lax.optimization_barrier((x,) + others)[0]


def shards(subs, blks, residual, stiffness, pattern, neumann_inv, dirichlet_inv, basis, node_ops, root_inv):
    here = lax.axis_index("sub")
    mine = lax.axis_index("blk")
    _, per, block, loads = residual.shape
    width = basis.shape[-1]
    coupled = pattern.shape[-1]
    levels = node_ops.shape[1]
    lanes = 128
    parts = loads // lanes
    assert per == 2 and levels > 2
    even = here % 2 == 0
    edge = (here == 0) | (here == subs - 1)
    upper = mine % 2 == 1
    flags = jnp.stack([even, edge, upper]).astype(jnp.int32)
    go = functools.partial(route, subs=subs, blks=blks)
    others = range(2, blks, 2)
    shape = jax.ShapeDtypeStruct
    half_shape = width, loads // 2
    small = 2 * width * width * loads // 2
    large = 10**11

    def swap(x, sub=0, blk=0):
        return go(x, target=lambda s, b: (s ^ sub, b ^ blk))

    def turned(x):
        return jnp.transpose(x[0], (1, 0, 2))

    modes = jnp.transpose(basis[0], (0, 2, 1))
    laid = jnp.transpose(residual[0].reshape(per, block, parts, lanes), (1, 2, 0, 3))

    given = modes, node_ops[0]
    modes, maps, scaled, keep, sent = call(
        start_kernel,
        tuple(shape(x.shape, x.dtype) for x in given)
        + (shape((per, block, loads), BF),)
        + (shape((2,) + half_shape, F32),) * 2,
        [SMEM] + [HBM] * (1 + len(given)),
        2 * per * block * width * loads,
        0,
        [pltpu.VMEM(laid.shape, F32), pltpu.SemaphoreType.DMA((1 + len(given),))],
        52,
    )(flags, laid, *given)
    got = swap(sent, blk=1)
    neumann = turned(neumann_inv)
    near_fix, far_fix, to_sibling, to_far = call(
        local_kernel,
        (shape((block, loads), F32),) * 2 + (shape((block, loads + width), BF),) * 2,
        [SMEM, VMEM, HBM, VMEM],
        large,
        0,
        [pltpu.VMEM(neumann.shape, BF), pltpu.SemaphoreType.DMA(())],
        16,
    )(flags, after(scaled, got), neumann, modes)
    half_bf, mapped_bf = (keep[0] + got[0]).astype(BF), (keep[1] + got[1]).astype(BF)

    same = jnp.stack([swap(half_bf, blk=d) for d in others])
    cross = jnp.stack([swap(mapped_bf, sub=1, blk=d) for d in (0,) + tuple(others)])
    coarse, value, own, own_bf, pack = call(
        pair_kernel,
        (shape(half_shape, F32),) * 3
        + (shape(half_shape, BF), shape((width, loads // 2 + width), BF)),
        [VMEM] * 5,
        3 * small,
        8 * width * width,
    )(keep, got, same, cross, maps)
    to_sibling, to_far = after(to_sibling, own_bf), after(to_far, own_bf)
    from_sibling = swap(to_sibling, sub=1)
    from_others = jnp.stack([swap(to_far, blk=d) for d in others])
    pack = swap(pack, sub=1)
    values = [value]
    for level in range(2, levels):
        value, own, own_bf = call(
            functools.partial(level_kernel, level),
            (shape(half_shape, F32),) * 2 + (shape(half_shape, BF),),
            [VMEM] * 3,
            small,
            4 * width * width,
        )(own, swap(own_bf, sub=2 ** (level - 1)), maps)
        values.append(value)
    fields = call(
        down_kernel,
        shape((2,) + half_shape, BF),
        [VMEM] * (6 + len(values)),
        (levels + 3) * small,
        4 * (levels + 2) * width * width,
    )(own, swap(own_bf, sub=subs // 2), pack, maps, root_inv, coarse, *values)
    far_id = jnp.where(even, 0, per - 1)
    matrix = lax.dynamic_index_in_dim(stiffness[0], after(far_id, own_bf), 0, False)
    fields, from_sibling, from_others, matrix = lax.optimization_barrier(
        (fields, from_sibling, from_others, matrix)
    )
    across = swap(fields, blk=1)
    fields = jnp.concatenate(
        [jnp.where(upper, across, fields), jnp.where(upper, fields, across)], axis=2
    )

    count = 2 + len(others)
    near, far, near_bf, mine_bf = call(
        face_kernel,
        (shape((block, loads), F32),) * 2
        + (shape((block, loads), BF), shape((count, block, loads), BF)),
        [SMEM] + [VMEM] * 7,
        2 * (count + 1) * block * width * loads,
        count * block * loads * 8,
    )(flags, fields, to_sibling, to_far, from_sibling, from_others, near_fix, far_fix)

    late = jnp.stack([swap(near_bf, blk=d) for d in others])
    core = swap(mine_bf, blk=1)
    far_in = go(
        after(mine_bf[0], core),
        target=lambda s, b: (s - 1 if s % 2 == 0 else s + 1, b),
    )
    columns = pattern[0, far_id]
    offset = (columns // per) ^ mine
    is_near = columns % per != far_id
    distant = offset // 2
    slots = jnp.where(
        is_near & (distant > 0),
        2 * count + (offset % 2) * len(others) + distant - 1,
        (offset % 2) * count + jnp.where(is_near, 1, jnp.where(distant > 0, 1 + distant, 0)),
    )
    first = 2 * count
    more = 2 * len(others)
    lists = pltpu.SMEM((2, -(-coupled // 4) * 4), jnp.int32)
    total, picked = call(
        couple_kernel,
        (shape((block, loads), F32), shape((block, block), BF)),
        [SMEM, SMEM] + [VMEM] * 4,
        large,
        2 * coupled * block * block,
        [pltpu.VMEM((first + 1, block, loads), BF), lists],
    )(slots, flags, matrix, turned(dirichlet_inv), mine_bf, core)
    late, total = lax.optimization_barrier((late, total))
    late_core = swap(late, blk=1)
    result = call(
        lambda slots_ref, flags_ref, *refs: finish_kernel(slots_ref, flags_ref, first, *refs),
        shape((block, parts, per, lanes), F32),
        [SMEM, SMEM] + [VMEM] * 8,
        2 * block * block * loads,
        block * loads * 16,
        [
            pltpu.VMEM((block, loads), F32),
            pltpu.VMEM((more + 1, block, loads), BF),
            lists,
        ],
    )(slots, flags, matrix, picked, total, late, late_core, far, far_in, near)
    return jnp.transpose(result, (2, 0, 1, 3)).reshape(per, block, loads)[None]


def solution(mesh):
    placed = (
        P("sub", "blk", None, None),
        P("sub", "blk", None, None, None),
        P("sub", "blk", None),
        P("sub", "blk", None, None),
        P("sub", "blk", None, None),
        P("sub", "blk", None, None),
        P("sub", None, None, None),
        P(),
    )
    return jax.shard_map(
        functools.partial(shards, mesh.shape["sub"], mesh.shape["blk"]),
        mesh=mesh,
        in_specs=placed,
        out_specs=P("sub", "blk", None, None),
        check_vma=False,
    )
```

```python
import functools

import jax
import jax.numpy as jnp
from jax import lax
from jax.experimental import pallas as pl
from jax.experimental.pallas import tpu as pltpu
from jax.sharding import PartitionSpec as P

BF = jnp.bfloat16
F32 = jnp.float32
VMEM = pl.BlockSpec(memory_space=pltpu.VMEM)
SMEM = pl.BlockSpec(memory_space=pltpu.SMEM)
HBM = pl.BlockSpec(memory_space=pltpu.HBM)


def route(x, subs, blks, target):
    pairs = []
    for s in range(subs):
        for b in range(blks):
            to = target(s, b)
            if to is not None and 0 <= to[0] < subs:
                pairs.append((s * blks + b, to[0] * blks + to[1]))
    return lax.ppermute(x, ("sub", "blk"), pairs)


def product(a, b, dims):
    a_high, b_high = a.astype(BF), b.astype(BF)
    a_low, b_low = (a - a_high.astype(F32)).astype(BF), (b - b_high.astype(F32)).astype(BF)
    part = functools.partial(
        lax.dot_general, dimension_numbers=(dims, ((), ())), preferred_element_type=F32
    )
    return part(a_high, b_high) + (part(a_high, b_low) + part(a_low, b_high))


def dot(a, b):
    return product(a, b, ((1,), (0,)))


def tdot(a, b):
    return product(a, b, ((0,), (0,)))


def bdot(a, b):
    return jnp.dot(a, b, preferred_element_type=F32)


def call(kernel, outs, specs, flops, moved, scratch=(), limit=16):
    return pl.pallas_call(
        kernel,
        out_shape=outs,
        in_specs=specs,
        out_specs=jax.tree.map(lambda _: VMEM, outs),
        scratch_shapes=scratch,
        compiler_params=pltpu.CompilerParams(vmem_limit_bytes=limit * 2**20),
        cost_estimate=pl.CostEstimate(flops=flops, bytes_accessed=moved, transcendentals=0),
    )


def rows_of(ref, j, part):
    rows, parts, blocks, lanes = ref.shape
    flat = ref.reshape(rows * parts * blocks, lanes)
    return flat, pl.ds(part * blocks + j, rows, stride=parts * blocks)


def start_kernel(flags_ref, residual_hbm, *refs):
    given = (len(refs) - 5) // 2
    sources, loaded = refs[:given], refs[given : 2 * given]
    scaled_ref, keep_ref, send_ref, residual_ref, sems = refs[2 * given :]
    modes_ref, maps_ref = loaded[:2]
    copies = [
        pltpu.make_async_copy(source, target, sems.at[i])
        for i, (source, target) in enumerate(zip((residual_hbm,) + sources, (residual_ref,) + loaded))
    ]
    for copy in copies:
        copy.start()
    is_even, is_edge, is_upper = (flags_ref[i] > 0 for i in range(3))
    per, _, loads = scaled_ref.shape
    lanes = residual_ref.shape[-1]
    total = jnp.zeros((modes_ref.shape[1], loads), F32)
    copies[0].wait()
    copies[1].wait()
    for j in range(per):
        is_far = is_even if j == 0 else jnp.logical_not(is_even)
        scale = jnp.where(is_edge & is_far, 1.0, 0.5).astype(F32)
        for part in range(loads // lanes):
            flat, rows = rows_of(residual_ref, j, part)
            scaled_ref[j, :, part * lanes : (part + 1) * lanes] = (flat[rows, :] * scale).astype(BF)
        total += bdot(modes_ref[j], scaled_ref[j])
    copies[2].wait()
    mapped = tdot(maps_ref[0], total)
    for i, values in enumerate((total, mapped)):
        low, high = values[:, : loads // 2], values[:, loads // 2 :]
        keep_ref[i] = jnp.where(is_upper, high, low)
        send_ref[i] = jnp.where(is_upper, low, high)
    for copy in copies[3:]:
        copy.wait()


def local_kernel(flags_ref, scaled_ref, inverse_hbm, modes_ref, near_ref, far_ref, near_out, far_out, inverse_ref, sem):
    copy = pltpu.make_async_copy(inverse_hbm, inverse_ref, sem)
    copy.start()
    loads = scaled_ref.shape[-1]
    is_even = flags_ref[0] > 0
    low_modes, high_modes = (modes_ref[j].T for j in range(2))
    near_out[:, loads:] = jnp.where(is_even, high_modes, low_modes)
    far_out[:, loads:] = jnp.where(is_even, low_modes, high_modes)
    copy.wait()
    inverse = inverse_ref[...]
    low, high = (bdot(inverse[:, j, :], scaled_ref[j]) for j in range(2))
    near, far = jnp.where(is_even, high, low), jnp.where(is_even, low, high)
    near_ref[...] = near
    far_ref[...] = far
    near_out[:, :loads] = near.astype(BF)
    far_out[:, :loads] = far.astype(BF)


def pair_kernel(keep_ref, got_ref, same_ref, cross_ref, map_ref, coarse_ref, pair_ref, own_ref, sent_ref, share_ref):
    coarse = keep_ref[0] + got_ref[0]
    for i in range(same_ref.shape[0]):
        coarse += same_ref[i].astype(F32)
    pair = tdot(map_ref[0], coarse)
    for i in range(cross_ref.shape[0]):
        pair += cross_ref[i].astype(F32)
    own = tdot(map_ref[1], pair)
    coarse_ref[...] = coarse
    pair_ref[...] = pair
    own_ref[...] = own
    sent_ref[...] = own.astype(BF)
    share_ref[...] = coarse.astype(BF)


def offer_kernel(coarse_ref, near_ref, near_fix_ref, map_ref, out_ref):
    loads = near_fix_ref.shape[-1]
    modes = near_ref[:, loads:]
    out_ref[:, :loads] = (near_fix_ref[...] + bdot(modes, coarse_ref[...])).astype(BF)
    high = map_ref[0].astype(BF)
    low = (map_ref[0] - high.astype(F32)).astype(BF)
    out_ref[:, loads:] = (bdot(modes, high) + bdot(modes, low)).astype(BF)


def level_kernel(level, own_ref, got_ref, map_ref, value_ref, next_ref, sent_ref):
    value = own_ref[...] + got_ref[...].astype(F32)
    value_ref[...] = value
    following = tdot(map_ref[level], value)
    next_ref[...] = following
    sent_ref[...] = following.astype(BF)


def down_kernel(own_ref, got_ref, map_ref, root_ref, coarse_ref, *refs):
    values, fields_ref = refs[:-1], refs[-1]
    field = dot(root_ref[...], own_ref[...] + got_ref[...].astype(F32))
    for level in reversed(range(1, map_ref.shape[0])):
        field = dot(map_ref[level], field) + values[level - 1][...]
    fields_ref[0] = (dot(map_ref[0], field) + coarse_ref[...]).astype(BF)
    fields_ref[1] = field.astype(BF)


def face_kernel(flags_ref, fields_ref, near_ref, far_ref, near_in_ref, far_in_ref, near_fix_ref, far_fix_ref, near_out, far_out, near_bf, far_bf, mine_bf):
    loads = near_fix_ref.shape[-1]
    field = fields_ref[0]
    own = near_fix_ref[...] + bdot(near_ref[:, loads:], field)
    other = near_in_ref[:, :loads].astype(F32) + bdot(near_in_ref[:, loads:], fields_ref[1])
    near = 0.5 * own + 0.5 * other
    near_out[...] = near
    near_bf[...] = near.astype(BF)
    mine_bf[1] = near.astype(BF)
    scale = jnp.where(flags_ref[1] > 0, 1.0, 0.5).astype(F32)
    far = (far_fix_ref[...] + bdot(far_ref[:, loads:], field)) * scale
    far_out[...] = far
    far_bf[...] = far.astype(BF)
    mine_bf[0] = far.astype(BF)
    for i in range(far_in_ref.shape[0]):
        block = far_in_ref[i, :, :loads].astype(F32) + bdot(far_in_ref[i, :, loads:], field)
        mine_bf[2 + i] = (block * scale).astype(BF)


def gather_products(slots_ref, first, matrix_ref, sources, values_ref, list_ref, total, width):
    start = 0
    for source in sources:
        values_ref[start : start + source.shape[0]] = source[...]
        start += source.shape[0]
    values_ref[start] = jnp.zeros(values_ref.shape[1:], BF)
    number = matrix_ref.shape[0]
    for i in range(list_ref.shape[1]):
        list_ref[0, i], list_ref[1, i] = 0, start

    def note(k, found):
        slot = slots_ref[k] - first
        is_here = (slot >= 0) & (slot < start)

        @pl.when(is_here)
        def _():
            list_ref[0, found], list_ref[1, found] = k, slot

        return found + is_here.astype(jnp.int32)

    found = lax.fori_loop(0, number, note, 0)

    def add(step, carry):
        places = [step * width + i for i in range(width)]
        matrices = jnp.concatenate([matrix_ref[list_ref[0, at]] for at in places], axis=1)
        values = jnp.concatenate([values_ref[list_ref[1, at]] for at in places], axis=0)
        total[...] += bdot(matrices, values)
        return carry

    lax.fori_loop(0, (found + width - 1) // width, add, 0)


def pick_kernel(flags_ref, inverse_ref, picked_ref):
    inverse = inverse_ref[...]
    picked_ref[...] = jnp.where(flags_ref[0] > 0, inverse[:, 0, :], inverse[:, 1, :])


def couple_kernel(slots_ref, flags_ref, matrix_ref, mine_ref, core_ref, total_ref, values_ref, list_ref):
    @pl.when(flags_ref[1] > 0)
    def _():
        total_ref[...] = jnp.zeros(total_ref.shape, F32)
        gather_products(slots_ref, 0, matrix_ref, (mine_ref, core_ref), values_ref, list_ref, total_ref, 8)


def finish_kernel(slots_ref, flags_ref, first, matrix_ref, picked_ref, total_ref, late_ref, late_core_ref, far_ref, far_in_ref, near_ref, out_ref, sum_ref, values_ref, list_ref):
    is_even = flags_ref[0] > 0
    is_edge = flags_ref[1] > 0

    @pl.when(is_edge)
    def _():
        sum_ref[...] = total_ref[...]
        gather_products(slots_ref, first, matrix_ref, (late_ref, late_core_ref), values_ref, list_ref, sum_ref, 4)
        sum_ref[...] = far_ref[...] - bdot(picked_ref[...], sum_ref[...].astype(BF))

    @pl.when(jnp.logical_not(is_edge))
    def _():
        sum_ref[...] = far_ref[...] + far_in_ref[...].astype(F32)

    _, parts, _, lanes = out_ref.shape
    for part in range(parts):
        columns = slice(part * lanes, (part + 1) * lanes)
        far, near = sum_ref[:, columns], near_ref[:, columns]
        for j, values in enumerate((jnp.where(is_even, far, near), jnp.where(is_even, near, far))):
            flat, rows = rows_of(out_ref, j, part)
            flat[rows, :] = values


def after(x, *others):
    return lax.optimization_barrier((x,) + others)[0]


def shards(subs, blks, residual, stiffness, pattern, neumann_inv, dirichlet_inv, basis, node_ops, root_inv):
    here = lax.axis_index("sub")
    mine = lax.axis_index("blk")
    _, per, block, loads = residual.shape
    width = basis.shape[-1]
    coupled = pattern.shape[-1]
    levels = node_ops.shape[1]
    lanes = 128
    parts = loads // lanes
    assert per == 2 and levels > 2
    even = here % 2 == 0
    edge = (here == 0) | (here == subs - 1)
    upper = mine % 2 == 1
    flags = jnp.stack([even, edge, upper]).astype(jnp.int32)
    go = functools.partial(route, subs=subs, blks=blks)
    others = range(2, blks, 2)
    shape = jax.ShapeDtypeStruct
    half_shape = width, loads // 2
    small = 2 * width * width * loads // 2
    large = 10**11

    def swap(x, sub=0, blk=0):
        return go(x, target=lambda s, b: (s ^ sub, b ^ blk))

    def joined(x):
        other = swap(x, blk=1)
        return jnp.concatenate([jnp.where(upper, other, x), jnp.where(upper, x, other)], axis=-1)

    def turned(x):
        return jnp.transpose(x[0], (1, 0, 2))

    modes = jnp.transpose(basis[0], (0, 2, 1))
    laid = jnp.transpose(residual[0].reshape(per, block, parts, lanes), (1, 2, 0, 3))

    given = modes, node_ops[0]
    modes, maps, scaled, keep, sent = call(
        start_kernel,
        tuple(shape(x.shape, x.dtype) for x in given)
        + (shape((per, block, loads), BF),)
        + (shape((2,) + half_shape, F32),) * 2,
        [SMEM] + [HBM] * (1 + len(given)),
        2 * per * block * width * loads,
        0,
        [pltpu.VMEM(laid.shape, F32), pltpu.SemaphoreType.DMA((1 + len(given),))],
        52,
    )(flags, laid, *given)
    got = swap(sent, blk=1)
    neumann = turned(neumann_inv)
    near_fix, far_fix, to_sibling, to_far = call(
        local_kernel,
        (shape((block, loads), F32),) * 2 + (shape((block, loads + width), BF),) * 2,
        [SMEM, VMEM, HBM, VMEM],
        large,
        0,
        [pltpu.VMEM(neumann.shape, BF), pltpu.SemaphoreType.DMA(())],
        16,
    )(flags, after(scaled, got), neumann, modes)
    half_bf, mapped_bf = (keep[0] + got[0]).astype(BF), (keep[1] + got[1]).astype(BF)

    same = jnp.stack([swap(half_bf, blk=d) for d in others])
    cross = jnp.stack([swap(mapped_bf, sub=1, blk=d) for d in (0,) + tuple(others)])
    cross, to_sibling, to_far = lax.optimization_barrier((cross, to_sibling, to_far))
    coarse, value, own, own_bf, share = call(
        pair_kernel,
        (shape(half_shape, F32),) * 3
        + (shape(half_shape, BF),) * 2,
        [VMEM] * 5,
        3 * small,
        8 * width * width,
        limit=4,
    )(keep, got, same, cross, maps)
    offer = call(
        offer_kernel,
        shape(to_sibling.shape, BF),
        [VMEM] * 4,
        3 * 10**9,
        0,
    )(joined(share), to_sibling, near_fix, maps)
    from_sibling = swap(offer, sub=1)
    from_others = jnp.stack([swap(to_far, blk=d) for d in others])
    values = [value]
    for level in range(2, levels):
        value, own, own_bf = call(
            functools.partial(level_kernel, level),
            (shape(half_shape, F32),) * 2 + (shape(half_shape, BF),),
            [VMEM] * 3,
            2*10**9,
            4 * width * width,
            limit=4,
        )(own, swap(own_bf, sub=2 ** (level - 1)), maps)
        values.append(value)
    fields = call(
        down_kernel,
        shape((2,) + half_shape, BF),
        [VMEM] * (5 + len(values)),
        (levels + 3) * small,
        4 * (levels + 2) * width * width,
        limit=4,
    )(own, swap(own_bf, sub=subs // 2), maps, root_inv, coarse, *values)
    picked = call(
        pick_kernel,
        shape((block, block), BF),
        [SMEM, VMEM],
        2 * 10**9,
        0,
    )(after(flags, own_bf), turned(dirichlet_inv))
    fields, from_sibling, from_others, picked = lax.optimization_barrier(
        (fields, from_sibling, from_others, picked)
    )
    fields = joined(fields)

    count = 2 + len(others)
    near, far, near_bf, far_bf, mine_bf = call(
        face_kernel,
        (shape((block, loads), F32),) * 2
        + (shape((block, loads), BF),) * 2
        + (shape((count, block, loads), BF),),
        [SMEM] + [VMEM] * 7,
        2 * (count + 1) * block * width * loads,
        block * loads * 16,
    )(flags, fields, to_sibling, to_far, from_sibling, from_others, near_fix, far_fix)
    late = jnp.stack([swap(near_bf, blk=d) for d in others])

    core = swap(mine_bf, blk=1)
    far_id = jnp.where(even, 0, per - 1)
    matrix = lax.dynamic_index_in_dim(stiffness[0], after(far_id, core), 0, False)
    far_in = go(
        far_bf,
        target=lambda s, b: (s, b ^ 1) if s in (0, subs - 1) else (s - 1 if s % 2 == 0 else s + 1, b),
    )
    columns = pattern[0, far_id]
    offset = (columns // per) ^ mine
    is_near = columns % per != far_id
    distant = offset // 2
    slots = jnp.where(
        is_near & (distant > 0),
        2 * count + (offset % 2) * len(others) + distant - 1,
        (offset % 2) * count + jnp.where(is_near, 1, jnp.where(distant > 0, 1 + distant, 0)),
    )
    first = 2 * count
    more = 2 * len(others)
    lists = pltpu.SMEM((2, -(-coupled // 8) * 8), jnp.int32)
    total = call(
        couple_kernel,
        shape((block, loads), F32),
        [SMEM, SMEM] + [VMEM] * 3,
        10**6,
        2 * coupled * block * block,
        [pltpu.VMEM((first + 1, block, loads), BF), lists],
    )(slots, flags, matrix, mine_bf, core)
    late, total = lax.optimization_barrier((late, total))
    late_core = swap(late, blk=1)
    result = call(
        lambda slots_ref, flags_ref, *refs: finish_kernel(slots_ref, flags_ref, first, *refs),
        shape((block, parts, per, lanes), F32),
        [SMEM, SMEM] + [VMEM] * 8,
        2 * block * block * loads,
        block * loads * 16,
        [
            pltpu.VMEM((block, loads), F32),
            pltpu.VMEM((more + 1, block, loads), BF),
            lists,
        ],
    )(slots, flags, matrix, picked, total, late, late_core, far, far_in, near)
    return jnp.transpose(result, (2, 0, 1, 3)).reshape(per, block, loads)[None]


def solution(mesh):
    placed = (
        P("sub", "blk", None, None),
        P("sub", "blk", None, None, None),
        P("sub", "blk", None),
        P("sub", "blk", None, None),
        P("sub", "blk", None, None),
        P("sub", "blk", None, None),
        P("sub", None, None, None),
        P(),
    )
    return jax.shard_map(
        functools.partial(shards, mesh.shape["sub"], mesh.shape["blk"]),
        mesh=mesh,
        in_specs=placed,
        out_specs=P("sub", "blk", None, None),
        check_vma=False,
    )
```

```python
import functools

import jax
import jax.numpy as jnp
from jax import lax
from jax.experimental import pallas as pl
from jax.experimental.pallas import tpu as pltpu
from jax.sharding import PartitionSpec as P

BF = jnp.bfloat16
F32 = jnp.float32
VMEM = pl.BlockSpec(memory_space=pltpu.VMEM)
SMEM = pl.BlockSpec(memory_space=pltpu.SMEM)
HBM = pl.BlockSpec(memory_space=pltpu.HBM)


def route(x, subs, blks, target):
    pairs = []
    for s in range(subs):
        for b in range(blks):
            to = target(s, b)
            if to is not None and 0 <= to[0] < subs:
                pairs.append((s * blks + b, to[0] * blks + to[1]))
    return lax.ppermute(x, ("sub", "blk"), pairs)


def product(a, b, dims):
    a_high, b_high = a.astype(BF), b.astype(BF)
    a_low, b_low = (a - a_high.astype(F32)).astype(BF), (b - b_high.astype(F32)).astype(BF)
    part = functools.partial(
        lax.dot_general, dimension_numbers=(dims, ((), ())), preferred_element_type=F32
    )
    return part(a_high, b_high) + (part(a_high, b_low) + part(a_low, b_high))


def dot(a, b):
    return product(a, b, ((1,), (0,)))


def tdot(a, b):
    return product(a, b, ((0,), (0,)))


def bdot(a, b):
    return jnp.dot(a, b, preferred_element_type=F32)


def call(kernel, outs, specs, flops, moved, scratch=(), limit=16):
    return pl.pallas_call(
        kernel,
        out_shape=outs,
        in_specs=specs,
        out_specs=jax.tree.map(lambda _: VMEM, outs),
        scratch_shapes=scratch,
        compiler_params=pltpu.CompilerParams(vmem_limit_bytes=limit * 2**20),
        cost_estimate=pl.CostEstimate(flops=flops, bytes_accessed=moved, transcendentals=0),
    )


def rows_of(ref, j, part):
    rows, parts, blocks, lanes = ref.shape
    flat = ref.reshape(rows * parts * blocks, lanes)
    return flat, pl.ds(part * blocks + j, rows, stride=parts * blocks)


def start_kernel(flags_ref, residual_hbm, *refs):
    given = (len(refs) - 5) // 2
    sources, loaded = refs[:given], refs[given : 2 * given]
    scaled_ref, keep_ref, send_ref, residual_ref, sems = refs[2 * given :]
    modes_ref, maps_ref = loaded[:2]
    copies = [
        pltpu.make_async_copy(source, target, sems.at[i])
        for i, (source, target) in enumerate(zip((residual_hbm,) + sources, (residual_ref,) + loaded))
    ]
    for copy in copies:
        copy.start()
    is_even, is_edge, is_upper = (flags_ref[i] > 0 for i in range(3))
    per, _, loads = scaled_ref.shape
    lanes = residual_ref.shape[-1]
    total = jnp.zeros((modes_ref.shape[1], loads), F32)
    copies[0].wait()
    copies[1].wait()
    for j in range(per):
        is_far = is_even if j == 0 else jnp.logical_not(is_even)
        scale = jnp.where(is_edge & is_far, 1.0, 0.5).astype(F32)
        for part in range(loads // lanes):
            flat, rows = rows_of(residual_ref, j, part)
            scaled_ref[j, :, part * lanes : (part + 1) * lanes] = (flat[rows, :] * scale).astype(BF)
        total += bdot(modes_ref[j], scaled_ref[j])
    copies[2].wait()
    mapped = tdot(maps_ref[0], total)
    for i, values in enumerate((total, mapped)):
        low, high = values[:, : loads // 2], values[:, loads // 2 :]
        keep_ref[i] = jnp.where(is_upper, high, low)
        send_ref[i] = jnp.where(is_upper, low, high)
    for copy in copies[3:]:
        copy.wait()


def local_kernel(flags_ref, scaled_ref, inverse_hbm, modes_ref, near_ref, far_ref, near_out, far_out, inverse_ref, rows_ref, sem):
    copy = pltpu.make_async_copy(inverse_hbm, inverse_ref, sem)
    copy.start()
    loads = scaled_ref.shape[-1]
    is_even = flags_ref[0] > 0
    low_modes, high_modes = (modes_ref[j].T for j in range(2))
    near_out[:, loads:] = jnp.where(is_even, high_modes, low_modes)
    far_out[:, loads:] = jnp.where(is_even, low_modes, high_modes)
    copy.wait()
    rows, per, columns = inverse_ref.shape
    inverse = inverse_ref[...].reshape(rows * per, columns)
    lanes = rows_ref.shape[-1]
    products = [bdot(inverse, scaled_ref[j]) for j in range(per)]
    for part in range(loads // lanes):
        here = slice(part * lanes, (part + 1) * lanes)
        for j in range(per):
            rows_ref[j, part] = products[j][:, here]
        low, high = (rows_ref[j, part, pl.ds(j, rows, stride=per), :] for j in range(per))
        near, far = jnp.where(is_even, high, low), jnp.where(is_even, low, high)
        near_ref[:, here] = near
        far_ref[:, here] = far
        near_out[:, here] = near.astype(BF)
        far_out[:, here] = far.astype(BF)


def pair_kernel(keep_ref, got_ref, same_ref, cross_ref, map_ref, coarse_ref, pair_ref, own_ref, sent_ref, share_ref):
    coarse = keep_ref[0] + got_ref[0]
    for i in range(same_ref.shape[0]):
        coarse += same_ref[i].astype(F32)
    pair = tdot(map_ref[0], coarse)
    for i in range(cross_ref.shape[0]):
        pair += cross_ref[i].astype(F32)
    own = tdot(map_ref[1], pair)
    coarse_ref[...] = coarse
    pair_ref[...] = pair
    own_ref[...] = own
    sent_ref[...] = own.astype(BF)
    share_ref[...] = coarse.astype(BF)


def offer_kernel(coarse_ref, near_ref, near_fix_ref, map_ref, out_ref):
    loads = near_fix_ref.shape[-1]
    modes = near_ref[:, loads:]
    out_ref[:, :loads] = (near_fix_ref[...] + bdot(modes, coarse_ref[...])).astype(BF)
    high = map_ref[0].astype(BF)
    low = (map_ref[0] - high.astype(F32)).astype(BF)
    out_ref[:, loads:] = (bdot(modes, high) + bdot(modes, low)).astype(BF)


def level_kernel(level, own_ref, got_ref, map_ref, value_ref, next_ref, sent_ref):
    value = own_ref[...] + got_ref[...].astype(F32)
    value_ref[...] = value
    following = tdot(map_ref[level], value)
    next_ref[...] = following
    sent_ref[...] = following.astype(BF)


def down_kernel(own_ref, got_ref, map_ref, root_ref, coarse_ref, *refs):
    values, fields_ref = refs[:-1], refs[-1]
    field = dot(root_ref[...], own_ref[...] + got_ref[...].astype(F32))
    for level in reversed(range(1, map_ref.shape[0])):
        field = dot(map_ref[level], field) + values[level - 1][...]
    fields_ref[0] = (dot(map_ref[0], field) + coarse_ref[...]).astype(BF)
    fields_ref[1] = field.astype(BF)


def near_kernel(fields_ref, near_ref, near_in_ref, near_fix_ref, near_out, near_bf):
    loads = near_fix_ref.shape[-1]
    own = near_fix_ref[...] + bdot(near_ref[:, loads:], fields_ref[0])
    other = near_in_ref[:, :loads].astype(F32) + bdot(near_in_ref[:, loads:], fields_ref[1])
    near = 0.5 * own + 0.5 * other
    near_out[...] = near
    near_bf[...] = near.astype(BF)


def far_kernel(flags_ref, fields_ref, near_ref, far_ref, far_in_ref, far_fix_ref, far_out, far_bf, mine_bf):
    loads = far_fix_ref.shape[-1]
    field = fields_ref[0]
    scale = jnp.where(flags_ref[1] > 0, 1.0, 0.5).astype(F32)
    far = (far_fix_ref[...] + bdot(far_ref[:, loads:], field)) * scale
    far_out[...] = far
    far_bf[...] = far.astype(BF)
    mine_bf[0] = far.astype(BF)
    mine_bf[1] = near_ref[...]
    for i in range(far_in_ref.shape[0]):
        block = far_in_ref[i, :, :loads].astype(F32) + bdot(far_in_ref[i, :, loads:], field)
        mine_bf[2 + i] = (block * scale).astype(BF)


def gather_products(slots_ref, first, matrix_ref, sources, values_ref, list_ref, total, width):
    start = 0
    for source in sources:
        values_ref[start : start + source.shape[0]] = source[...]
        start += source.shape[0]
    values_ref[start] = jnp.zeros(values_ref.shape[1:], BF)
    number = matrix_ref.shape[0]
    for i in range(list_ref.shape[1]):
        list_ref[0, i], list_ref[1, i] = 0, start

    def note(k, found):
        slot = slots_ref[k] - first
        is_here = (slot >= 0) & (slot < start)

        @pl.when(is_here)
        def _():
            list_ref[0, found], list_ref[1, found] = k, slot

        return found + is_here.astype(jnp.int32)

    found = lax.fori_loop(0, number, note, 0)

    def add(step, carry):
        places = [step * width + i for i in range(width)]
        matrices = jnp.concatenate([matrix_ref[list_ref[0, at]] for at in places], axis=1)
        values = jnp.concatenate([values_ref[list_ref[1, at]] for at in places], axis=0)
        total[...] += bdot(matrices, values)
        return carry

    lax.fori_loop(0, (found + width - 1) // width, add, 0)


def pick_kernel(flags_ref, inverse_ref, picked_ref):
    inverse = inverse_ref[...]
    picked_ref[...] = jnp.where(flags_ref[0] > 0, inverse[:, 0, :], inverse[:, 1, :])


def couple_kernel(slots_ref, flags_ref, matrix_ref, mine_ref, core_ref, total_ref, values_ref, list_ref):
    @pl.when(flags_ref[1] > 0)
    def _():
        total_ref[...] = jnp.zeros(total_ref.shape, F32)
        gather_products(slots_ref, 0, matrix_ref, (mine_ref, core_ref), values_ref, list_ref, total_ref, 8)


def finish_kernel(slots_ref, flags_ref, first, matrix_ref, picked_ref, total_ref, late_ref, late_core_ref, far_ref, far_in_ref, near_ref, out_ref, sum_ref, values_ref, list_ref):
    is_even = flags_ref[0] > 0
    is_edge = flags_ref[1] > 0

    @pl.when(is_edge)
    def _():
        sum_ref[...] = total_ref[...]
        gather_products(slots_ref, first, matrix_ref, (late_ref, late_core_ref), values_ref, list_ref, sum_ref, 4)
        sum_ref[...] = far_ref[...] - bdot(picked_ref[...], sum_ref[...].astype(BF))

    @pl.when(jnp.logical_not(is_edge))
    def _():
        sum_ref[...] = far_ref[...] + far_in_ref[...].astype(F32)

    _, parts, _, lanes = out_ref.shape
    for part in range(parts):
        columns = slice(part * lanes, (part + 1) * lanes)
        far, near = sum_ref[:, columns], near_ref[:, columns]
        for j, values in enumerate((jnp.where(is_even, far, near), jnp.where(is_even, near, far))):
            flat, rows = rows_of(out_ref, j, part)
            flat[rows, :] = values


def after(x, *others):
    return lax.optimization_barrier((x,) + others)[0]


def shards(subs, blks, residual, stiffness, pattern, neumann_inv, dirichlet_inv, basis, node_ops, root_inv):
    here = lax.axis_index("sub")
    mine = lax.axis_index("blk")
    _, per, block, loads = residual.shape
    width = basis.shape[-1]
    coupled = pattern.shape[-1]
    levels = node_ops.shape[1]
    lanes = 128
    parts = loads // lanes
    assert per == 2 and levels > 2
    even = here % 2 == 0
    edge = (here == 0) | (here == subs - 1)
    upper = mine % 2 == 1
    flags = jnp.stack([even, edge, upper]).astype(jnp.int32)
    go = functools.partial(route, subs=subs, blks=blks)
    others = range(2, blks, 2)
    shape = jax.ShapeDtypeStruct
    half_shape = width, loads // 2
    small = 2 * width * width * loads // 2
    large = 10**11

    def swap(x, sub=0, blk=0):
        return go(x, target=lambda s, b: (s ^ sub, b ^ blk))

    def joined(x):
        other = swap(x, blk=1)
        return jnp.concatenate([jnp.where(upper, other, x), jnp.where(upper, x, other)], axis=-1)

    def turned(x):
        return jnp.transpose(x[0], (1, 0, 2))

    modes = jnp.transpose(basis[0], (0, 2, 1))
    laid = jnp.transpose(residual[0].reshape(per, block, parts, lanes), (1, 2, 0, 3))

    given = modes, node_ops[0]
    modes, maps, scaled, keep, sent = call(
        start_kernel,
        tuple(shape(x.shape, x.dtype) for x in given)
        + (shape((per, block, loads), BF),)
        + (shape((2,) + half_shape, F32),) * 2,
        [SMEM] + [HBM] * (1 + len(given)),
        2 * per * block * width * loads,
        0,
        [pltpu.VMEM(laid.shape, F32), pltpu.SemaphoreType.DMA((1 + len(given),))],
        52,
    )(flags, laid, *given)
    got = swap(sent, blk=1)
    neumann = turned(neumann_inv)
    near_fix, far_fix, to_sibling, to_far = call(
        local_kernel,
        (shape((block, loads), F32),) * 2 + (shape((block, loads + width), BF),) * 2,
        [SMEM, VMEM, HBM, VMEM],
        large,
        0,
        [
            pltpu.VMEM(neumann.shape, BF),
            pltpu.VMEM((per, parts, per * block, lanes), F32),
            pltpu.SemaphoreType.DMA(()),
        ],
        16,
    )(flags, after(scaled, got), neumann, modes)
    half_bf, mapped_bf = (keep[0] + got[0]).astype(BF), (keep[1] + got[1]).astype(BF)

    same = jnp.stack([swap(half_bf, blk=d) for d in others])
    cross = jnp.stack([swap(mapped_bf, sub=1, blk=d) for d in (0,) + tuple(others)])
    cross, to_sibling, to_far = lax.optimization_barrier((cross, to_sibling, to_far))
    coarse, value, own, own_bf, share = call(
        pair_kernel,
        (shape(half_shape, F32),) * 3
        + (shape(half_shape, BF),) * 2,
        [VMEM] * 5,
        3 * small,
        8 * width * width,
        limit=4,
    )(keep, got, same, cross, maps)
    offer = call(
        offer_kernel,
        shape(to_sibling.shape, BF),
        [VMEM] * 4,
        3 * 10**9,
        0,
    )(joined(share), to_sibling, near_fix, maps)
    from_sibling = swap(offer, sub=1)
    from_others = jnp.stack([swap(to_far, blk=d) for d in others])
    values = [value]
    for level in range(2, levels):
        value, own, own_bf = call(
            functools.partial(level_kernel, level),
            (shape(half_shape, F32),) * 2 + (shape(half_shape, BF),),
            [VMEM] * 3,
            2*10**9,
            4 * width * width,
            limit=4,
        )(own, swap(own_bf, sub=2 ** (level - 1)), maps)
        values.append(value)
    fields = call(
        down_kernel,
        shape((2,) + half_shape, BF),
        [VMEM] * (5 + len(values)),
        (levels + 3) * small,
        4 * (levels + 2) * width * width,
        limit=4,
    )(own, swap(own_bf, sub=subs // 2), maps, root_inv, coarse, *values)
    far_id = jnp.where(even, 0, per - 1)
    matrix = lax.dynamic_index_in_dim(stiffness[0], after(far_id, own_bf), 0, False)
    fields, from_sibling, from_others, matrix = lax.optimization_barrier(
        (fields, from_sibling, from_others, matrix)
    )
    fields = joined(fields)

    count = 2 + len(others)
    face = 2 * block * width * loads
    near, near_bf = call(
        near_kernel,
        (shape((block, loads), F32), shape((block, loads), BF)),
        [VMEM] * 4,
        2 * face,
        block * loads * 8,
    )(fields, to_sibling, from_sibling, near_fix)
    late = jnp.stack([swap(near_bf, blk=d) for d in others])
    far, far_bf, mine_bf = call(
        far_kernel,
        (shape((block, loads), F32), shape((block, loads), BF), shape((count, block, loads), BF)),
        [SMEM] + [VMEM] * 5,
        10**11,
        count * block * loads * 8,
    )(flags, fields, near_bf, to_far, from_others, far_fix)

    core = swap(mine_bf, blk=1)
    picked = call(
        pick_kernel,
        shape((block, block), BF),
        [SMEM, VMEM],
        1000,
        0,
    )(after(flags, near_bf), turned(dirichlet_inv))
    far_in = go(
        far_bf,
        target=lambda s, b: (s, b ^ 1) if s in (0, subs - 1) else (s - 1 if s % 2 == 0 else s + 1, b),
    )
    columns = pattern[0, far_id]
    offset = (columns // per) ^ mine
    is_near = columns % per != far_id
    distant = offset // 2
    slots = jnp.where(
        is_near & (distant > 0),
        2 * count + (offset % 2) * len(others) + distant - 1,
        (offset % 2) * count + jnp.where(is_near, 1, jnp.where(distant > 0, 1 + distant, 0)),
    )
    first = 2 * count
    more = 2 * len(others)
    lists = pltpu.SMEM((2, -(-coupled // 8) * 8), jnp.int32)
    total = call(
        couple_kernel,
        shape((block, loads), F32),
        [SMEM, SMEM] + [VMEM] * 3,
        1000,
        2 * coupled * block * block,
        [pltpu.VMEM((first + 1, block, loads), BF), lists],
    )(slots, flags, matrix, mine_bf, core)
    late, total, picked = lax.optimization_barrier((late, total, picked))
    late_core = swap(late, blk=1)
    result = call(
        lambda slots_ref, flags_ref, *refs: finish_kernel(slots_ref, flags_ref, first, *refs),
        shape((block, parts, per, lanes), F32),
        [SMEM, SMEM] + [VMEM] * 8,
        2 * block * block * loads,
        block * loads * 16,
        [
            pltpu.VMEM((block, loads), F32),
            pltpu.VMEM((more + 1, block, loads), BF),
            lists,
        ],
    )(slots, flags, matrix, picked, total, late, late_core, far, far_in, near)
    return jnp.transpose(result, (2, 0, 1, 3)).reshape(per, block, loads)[None]


def solution(mesh):
    placed = (
        P("sub", "blk", None, None),
        P("sub", "blk", None, None, None),
        P("sub", "blk", None),
        P("sub", "blk", None, None),
        P("sub", "blk", None, None),
        P("sub", "blk", None, None),
        P("sub", None, None, None),
        P(),
    )
    return jax.shard_map(
        functools.partial(shards, mesh.shape["sub"], mesh.shape["blk"]),
        mesh=mesh,
        in_specs=placed,
        out_specs=P("sub", "blk", None, None),
        check_vma=False,
    )
```

```python
import functools

import jax
import jax.numpy as jnp
from jax import lax
from jax.experimental import pallas as pl
from jax.experimental.pallas import tpu as pltpu
from jax.sharding import PartitionSpec as P

BF = jnp.bfloat16
F32 = jnp.float32
VMEM = pl.BlockSpec(memory_space=pltpu.VMEM)
SMEM = pl.BlockSpec(memory_space=pltpu.SMEM)
HBM = pl.BlockSpec(memory_space=pltpu.HBM)


def route(x, subs, blks, target):
    pairs = []
    for s in range(subs):
        for b in range(blks):
            to = target(s, b)
            if to is not None and 0 <= to[0] < subs:
                pairs.append((s * blks + b, to[0] * blks + to[1]))
    return lax.ppermute(x, ("sub", "blk"), pairs)


def product(a, b, dims):
    a_high, b_high = a.astype(BF), b.astype(BF)
    a_low, b_low = (a - a_high.astype(F32)).astype(BF), (b - b_high.astype(F32)).astype(BF)
    part = functools.partial(
        lax.dot_general, dimension_numbers=(dims, ((), ())), preferred_element_type=F32
    )
    return part(a_high, b_high) + (part(a_high, b_low) + part(a_low, b_high))


def dot(a, b):
    return product(a, b, ((1,), (0,)))


def tdot(a, b):
    return product(a, b, ((0,), (0,)))


def bdot(a, b):
    return jnp.dot(a, b, preferred_element_type=F32)


def call(kernel, outs, specs, flops, moved, scratch=(), limit=16, outs_at=None):
    return pl.pallas_call(
        kernel,
        out_shape=outs,
        in_specs=specs,
        out_specs=jax.tree.map(lambda _: VMEM, outs) if outs_at is None else outs_at,
        scratch_shapes=scratch,
        compiler_params=pltpu.CompilerParams(vmem_limit_bytes=limit * 2**20),
        cost_estimate=pl.CostEstimate(flops=flops, bytes_accessed=moved, transcendentals=0),
    )


def rows_of(ref, j, part):
    rows, parts, blocks, lanes = ref.shape
    flat = ref.reshape(rows * parts * blocks, lanes)
    return flat, pl.ds(part * blocks + j, rows, stride=parts * blocks)


def start_kernel(flags_ref, residual_hbm, *refs):
    given = (len(refs) - 5) // 2
    sources, loaded = refs[:given], refs[given : 2 * given]
    scaled_ref, keep_ref, send_ref, residual_ref, sems = refs[2 * given :]
    modes_ref, maps_ref = loaded[:2]
    copies = [
        pltpu.make_async_copy(source, target, sems.at[i])
        for i, (source, target) in enumerate(zip((residual_hbm,) + sources, (residual_ref,) + loaded))
    ]
    for copy in copies:
        copy.start()
    is_even, is_edge, is_upper = (flags_ref[i] > 0 for i in range(3))
    per, _, loads = scaled_ref.shape
    lanes = residual_ref.shape[-1]
    total = jnp.zeros((modes_ref.shape[1], loads), F32)
    copies[0].wait()
    copies[1].wait()
    for j in range(per):
        is_far = is_even if j == 0 else jnp.logical_not(is_even)
        scale = jnp.where(is_edge & is_far, 1.0, 0.5).astype(F32)
        for part in range(loads // lanes):
            flat, rows = rows_of(residual_ref, j, part)
            scaled_ref[j, :, part * lanes : (part + 1) * lanes] = (flat[rows, :] * scale).astype(BF)
        total += bdot(modes_ref[j], scaled_ref[j])
    copies[2].wait()
    mapped = tdot(maps_ref[0], total)
    for i, values in enumerate((total, mapped)):
        low, high = values[:, : loads // 2], values[:, loads // 2 :]
        keep_ref[i] = jnp.where(is_upper, high, low)
        send_ref[i] = jnp.where(is_upper, low, high)
    for copy in copies[3:]:
        copy.wait()


def local_kernel(flags_ref, scaled_ref, inverse_hbm, modes_ref, near_ref, far_ref, near_out, far_out, inverse_ref, rows_ref, sem):
    copy = pltpu.make_async_copy(inverse_hbm, inverse_ref, sem)
    copy.start()
    loads = scaled_ref.shape[-1]
    is_even = flags_ref[0] > 0
    low_modes, high_modes = (modes_ref[j].T for j in range(2))
    near_out[:, loads:] = jnp.where(is_even, high_modes, low_modes)
    far_out[:, loads:] = jnp.where(is_even, low_modes, high_modes)
    copy.wait()
    rows, per, columns = inverse_ref.shape
    inverse = inverse_ref[...].reshape(rows * per, columns)
    lanes = rows_ref.shape[-1]
    products = [bdot(inverse, scaled_ref[j]) for j in range(per)]
    for part in range(loads // lanes):
        here = slice(part * lanes, (part + 1) * lanes)
        for j in range(per):
            rows_ref[j, part] = products[j][:, here]
        low, high = (rows_ref[j, part, pl.ds(j, rows, stride=per), :] for j in range(per))
        near, far = jnp.where(is_even, high, low), jnp.where(is_even, low, high)
        near_ref[:, here] = near
        far_ref[:, here] = far
        near_out[:, here] = near.astype(BF)
        far_out[:, here] = far.astype(BF)


def pair_kernel(keep_ref, got_ref, same_ref, cross_ref, map_ref, coarse_ref, pair_ref, own_ref, sent_ref, share_ref):
    coarse = keep_ref[0] + got_ref[0]
    for i in range(same_ref.shape[0]):
        coarse += same_ref[i].astype(F32)
    pair = tdot(map_ref[0], coarse)
    for i in range(cross_ref.shape[0]):
        pair += cross_ref[i].astype(F32)
    own = tdot(map_ref[1], pair)
    coarse_ref[...] = coarse
    pair_ref[...] = pair
    own_ref[...] = own
    sent_ref[...] = own.astype(BF)
    share_ref[...] = coarse.astype(BF)


def offer_kernel(coarse_ref, near_ref, near_fix_ref, map_ref, out_ref):
    loads = near_fix_ref.shape[-1]
    modes = near_ref[:, loads:]
    out_ref[:, :loads] = (near_fix_ref[...] + bdot(modes, coarse_ref[...])).astype(BF)
    high = map_ref[0].astype(BF)
    low = (map_ref[0] - high.astype(F32)).astype(BF)
    out_ref[:, loads:] = (bdot(modes, high) + bdot(modes, low)).astype(BF)


def level_kernel(level, own_ref, got_ref, map_ref, value_ref, next_ref, sent_ref):
    value = own_ref[...] + got_ref[...].astype(F32)
    value_ref[...] = value
    following = tdot(map_ref[level], value)
    next_ref[...] = following
    sent_ref[...] = following.astype(BF)


def down_kernel(own_ref, got_ref, map_ref, root_ref, coarse_ref, *refs):
    values, fields_ref = refs[:-1], refs[-1]
    field = dot(root_ref[...], own_ref[...] + got_ref[...].astype(F32))
    for level in reversed(range(1, map_ref.shape[0])):
        field = dot(map_ref[level], field) + values[level - 1][...]
    fields_ref[0] = (dot(map_ref[0], field) + coarse_ref[...]).astype(BF)
    fields_ref[1] = field.astype(BF)


def near_kernel(fields_ref, near_ref, near_in_ref, near_fix_ref, near_out, near_bf):
    loads = near_fix_ref.shape[-1]
    own = near_fix_ref[...] + bdot(near_ref[:, loads:], fields_ref[0])
    other = near_in_ref[:, :loads].astype(F32) + bdot(near_in_ref[:, loads:], fields_ref[1])
    near = 0.5 * own + 0.5 * other
    near_out[...] = near
    near_bf[...] = near.astype(BF)


def far_kernel(flags_ref, fields_ref, near_ref, far_ref, far_in_ref, far_fix_ref, far_out, far_bf, mine_bf):
    loads = far_fix_ref.shape[-1]
    field = fields_ref[0]
    scale = jnp.where(flags_ref[1] > 0, 1.0, 0.5).astype(F32)
    far = (far_fix_ref[...] + bdot(far_ref[:, loads:], field)) * scale
    far_out[...] = far
    far_bf[...] = far.astype(BF)
    mine_bf[0] = far.astype(BF)
    mine_bf[1] = near_ref[...]
    for i in range(far_in_ref.shape[0]):
        block = far_in_ref[i, :, :loads].astype(F32) + bdot(far_in_ref[i, :, loads:], field)
        mine_bf[2 + i] = (block * scale).astype(BF)


def note_slots(slots_ref, first, end, number, list_ref):
    for i in range(list_ref.shape[1]):
        list_ref[0, i], list_ref[1, i] = 0, end - first

    def note(k, found):
        slot = slots_ref[k] - first
        is_here = (slot >= 0) & (slot < end - first)

        @pl.when(is_here)
        def _():
            list_ref[0, found], list_ref[1, found] = k, slot

        return found + is_here.astype(jnp.int32)

    list_ref[2, 0] = lax.fori_loop(0, number, note, 0)


def add_products(list_ref, matrix_ref, sources, values_ref, total):
    end = 0
    for source in sources:
        values_ref[end : end + source.shape[0]] = source[...]
        end += source.shape[0]
    values_ref[end] = jnp.zeros(values_ref.shape[1:], BF)
    found = list_ref[2, 0]
    most = 8

    def add(first, width):
        places = [first + i for i in range(width)]
        matrices = jnp.concatenate([matrix_ref[list_ref[0, at]] for at in places], axis=1)
        values = jnp.concatenate([values_ref[list_ref[1, at]] for at in places], axis=0)
        total[...] += bdot(matrices, values)

    def whole(step, carry):
        add(step * most, most)
        return carry

    steps = found // most
    lax.fori_loop(0, steps, whole, 0)
    left = found - steps * most
    for width in range(2, most + 1, 2):

        @pl.when((left > width - 2) & (left <= width))
        def _():
            add(steps * most, width)


def pick_kernel(flags_ref, inverse_ref, picked_ref):
    inverse = inverse_ref[...]
    picked_ref[...] = jnp.where(flags_ref[0] > 0, inverse[:, 0, :], inverse[:, 1, :])


def couple_kernel(late, slots_ref, flags_ref, matrix_ref, mine_ref, core_ref, total_ref, late_list_ref, values_ref, list_ref):
    @pl.when(flags_ref[1] > 0)
    def _():
        total_ref[...] = jnp.zeros(total_ref.shape, F32)
        sources = mine_ref, core_ref
        here = sum(source.shape[0] for source in sources)
        number = matrix_ref.shape[0]
        note_slots(slots_ref, 0, here, number, list_ref)
        note_slots(slots_ref, here, here + late, number, late_list_ref)
        add_products(list_ref, matrix_ref, sources, values_ref, total_ref)


def finish_kernel(list_ref, flags_ref, matrix_ref, picked_ref, total_ref, late_ref, late_core_ref, far_ref, far_in_ref, near_ref, out_ref, sum_ref, values_ref):
    is_even = flags_ref[0] > 0
    is_edge = flags_ref[1] > 0

    @pl.when(is_edge)
    def _():
        sum_ref[...] = total_ref[...]
        add_products(list_ref, matrix_ref, (late_ref, late_core_ref), values_ref, sum_ref)
        sum_ref[...] = far_ref[...] - bdot(picked_ref[...], sum_ref[...].astype(BF))

    @pl.when(jnp.logical_not(is_edge))
    def _():
        sum_ref[...] = far_ref[...] + far_in_ref[...].astype(F32)

    _, parts, _, lanes = out_ref.shape
    for part in range(parts):
        columns = slice(part * lanes, (part + 1) * lanes)
        far, near = sum_ref[:, columns], near_ref[:, columns]
        for j, values in enumerate((jnp.where(is_even, far, near), jnp.where(is_even, near, far))):
            flat, rows = rows_of(out_ref, j, part)
            flat[rows, :] = values


def after(x, *others):
    return lax.optimization_barrier((x,) + others)[0]


def shards(subs, blks, residual, stiffness, pattern, neumann_inv, dirichlet_inv, basis, node_ops, root_inv):
    here = lax.axis_index("sub")
    mine = lax.axis_index("blk")
    _, per, block, loads = residual.shape
    width = basis.shape[-1]
    coupled = pattern.shape[-1]
    levels = node_ops.shape[1]
    lanes = 128
    parts = loads // lanes
    assert per == 2 and levels > 2
    even = here % 2 == 0
    edge = (here == 0) | (here == subs - 1)
    upper = mine % 2 == 1
    flags = jnp.stack([even, edge, upper]).astype(jnp.int32)
    go = functools.partial(route, subs=subs, blks=blks)
    others = range(2, blks, 2)
    shape = jax.ShapeDtypeStruct
    half_shape = width, loads // 2
    small = 2 * width * width * loads // 2
    large = 10**11

    def swap(x, sub=0, blk=0):
        return go(x, target=lambda s, b: (s ^ sub, b ^ blk))

    def joined(x):
        other = swap(x, blk=1)
        return jnp.concatenate([jnp.where(upper, other, x), jnp.where(upper, x, other)], axis=-1)

    def turned(x):
        return jnp.transpose(x[0], (1, 0, 2))

    modes = jnp.transpose(basis[0], (0, 2, 1))
    laid = jnp.transpose(residual[0].reshape(per, block, parts, lanes), (1, 2, 0, 3))

    given = modes, node_ops[0]
    modes, maps, scaled, keep, sent = call(
        start_kernel,
        tuple(shape(x.shape, x.dtype) for x in given)
        + (shape((per, block, loads), BF),)
        + (shape((2,) + half_shape, F32),) * 2,
        [SMEM] + [HBM] * (1 + len(given)),
        2 * per * block * width * loads,
        0,
        [pltpu.VMEM(laid.shape, F32), pltpu.SemaphoreType.DMA((1 + len(given),))],
        52,
    )(flags, laid, *given)
    got = swap(sent, blk=1)
    neumann = turned(neumann_inv)
    near_fix, far_fix, to_sibling, to_far = call(
        local_kernel,
        (shape((block, loads), F32),) * 2 + (shape((block, loads + width), BF),) * 2,
        [SMEM, VMEM, HBM, VMEM],
        large,
        0,
        [
            pltpu.VMEM(neumann.shape, BF),
            pltpu.VMEM((per, parts, per * block, lanes), F32),
            pltpu.SemaphoreType.DMA(()),
        ],
        16,
    )(flags, after(scaled, got), neumann, modes)
    half_bf, mapped_bf = (keep[0] + got[0]).astype(BF), (keep[1] + got[1]).astype(BF)

    same = jnp.stack([swap(half_bf, blk=d) for d in others])
    cross = jnp.stack([swap(mapped_bf, sub=1, blk=d) for d in (0,) + tuple(others)])
    cross, to_sibling, to_far = lax.optimization_barrier((cross, to_sibling, to_far))
    coarse, value, own, own_bf, share = call(
        pair_kernel,
        (shape(half_shape, F32),) * 3
        + (shape(half_shape, BF),) * 2,
        [VMEM] * 5,
        3 * small,
        8 * width * width,
        limit=4,
    )(keep, got, same, cross, maps)
    offer = call(
        offer_kernel,
        shape(to_sibling.shape, BF),
        [VMEM] * 4,
        3 * 10**9,
        0,
    )(joined(share), to_sibling, near_fix, maps)
    from_sibling = swap(offer, sub=1)
    from_others = jnp.stack([swap(to_far, blk=d) for d in others])
    values = [value]
    for level in range(2, levels):
        value, own, own_bf = call(
            functools.partial(level_kernel, level),
            (shape(half_shape, F32),) * 2 + (shape(half_shape, BF),),
            [VMEM] * 3,
            2*10**9,
            4 * width * width,
            limit=4,
        )(own, swap(own_bf, sub=2 ** (level - 1)), maps)
        values.append(value)
    fields = call(
        down_kernel,
        shape((2,) + half_shape, BF),
        [VMEM] * (5 + len(values)),
        (levels + 3) * small,
        4 * (levels + 2) * width * width,
        limit=4,
    )(own, swap(own_bf, sub=subs // 2), maps, root_inv, coarse, *values)
    far_id = jnp.where(even, 0, per - 1)
    matrix = lax.dynamic_index_in_dim(stiffness[0], after(far_id, own_bf), 0, False)
    fields, from_sibling, from_others, matrix = lax.optimization_barrier(
        (fields, from_sibling, from_others, matrix)
    )
    fields = joined(fields)

    count = 2 + len(others)
    face = 2 * block * width * loads
    near, near_bf = call(
        near_kernel,
        (shape((block, loads), F32), shape((block, loads), BF)),
        [VMEM] * 4,
        2 * face,
        block * loads * 8,
    )(fields, to_sibling, from_sibling, near_fix)
    late = jnp.stack(
        [
            go(near_bf, target=lambda s, b, d=d: (s, b ^ d) if s in (0, subs - 1) else (s, b ^ 1))
            for d in others
        ]
    )
    far, far_bf, mine_bf = call(
        far_kernel,
        (shape((block, loads), F32), shape((block, loads), BF), shape((count, block, loads), BF)),
        [SMEM] + [VMEM] * 5,
        10**11,
        count * block * loads * 8,
    )(flags, fields, near_bf, to_far, from_others, far_fix)

    core = swap(mine_bf, blk=1)
    picked = call(
        pick_kernel,
        shape((block, block), BF),
        [SMEM, VMEM],
        1000,
        0,
    )(after(flags, near_bf), turned(dirichlet_inv))
    far_in = go(
        far_bf,
        target=lambda s, b: (s, b ^ 1) if s in (0, subs - 1) else (s - 1 if s % 2 == 0 else s + 1, b),
    )
    columns = pattern[0, far_id]
    offset = (columns // per) ^ mine
    is_near = columns % per != far_id
    distant = offset // 2
    slots = jnp.where(
        is_near & (distant > 0),
        2 * count + (offset % 2) * len(others) + distant - 1,
        (offset % 2) * count + jnp.where(is_near, 1, jnp.where(distant > 0, 1 + distant, 0)),
    )
    first = 2 * count
    more = 2 * len(others)
    listed = (3, -(-coupled // 8) * 8)
    total, late_list = call(
        functools.partial(couple_kernel, more),
        (shape((block, loads), F32), shape(listed, jnp.int32)),
        [SMEM, SMEM] + [VMEM] * 3,
        1000,
        2 * coupled * block * block,
        [pltpu.VMEM((first + 1, block, loads), BF), pltpu.SMEM(listed, jnp.int32)],
        outs_at=(VMEM, SMEM),
    )(slots, flags, matrix, mine_bf, core)
    late, total, picked = lax.optimization_barrier((late, total, picked))
    late_core = swap(late, blk=1)
    result = call(
        finish_kernel,
        shape((block, parts, per, lanes), F32),
        [SMEM, SMEM] + [VMEM] * 8,
        2 * block * block * loads,
        block * loads * 16,
        [
            pltpu.VMEM((block, loads), F32),
            pltpu.VMEM((more + 1, block, loads), BF),
        ],
    )(late_list, flags, matrix, picked, total, late, late_core, far, far_in, near)
    return jnp.transpose(result, (2, 0, 1, 3)).reshape(per, block, loads)[None]


def solution(mesh):
    placed = (
        P("sub", "blk", None, None),
        P("sub", "blk", None, None, None),
        P("sub", "blk", None),
        P("sub", "blk", None, None),
        P("sub", "blk", None, None),
        P("sub", "blk", None, None),
        P("sub", None, None, None),
        P(),
    )
    return jax.shard_map(
        functools.partial(shards, mesh.shape["sub"], mesh.shape["blk"]),
        mesh=mesh,
        in_specs=placed,
        out_specs=P("sub", "blk", None, None),
        check_vma=False,
    )
```

```python
import functools

import jax
import jax.numpy as jnp
from jax import lax
from jax.experimental import pallas as pl
from jax.experimental.pallas import tpu as pltpu
from jax.sharding import PartitionSpec as P

BF = jnp.bfloat16
F32 = jnp.float32
VMEM = pl.BlockSpec(memory_space=pltpu.VMEM)
SMEM = pl.BlockSpec(memory_space=pltpu.SMEM)
HBM = pl.BlockSpec(memory_space=pltpu.HBM)


def route(x, subs, blks, target):
    pairs = []
    for s in range(subs):
        for b in range(blks):
            to = target(s, b)
            if to is not None and 0 <= to[0] < subs:
                pairs.append((s * blks + b, to[0] * blks + to[1]))
    return lax.ppermute(x, ("sub", "blk"), pairs)


def product(a, b, dims):
    a_high, b_high = a.astype(BF), b.astype(BF)
    a_low, b_low = (a - a_high.astype(F32)).astype(BF), (b - b_high.astype(F32)).astype(BF)
    part = functools.partial(
        lax.dot_general, dimension_numbers=(dims, ((), ())), preferred_element_type=F32
    )
    return part(a_high, b_high) + (part(a_high, b_low) + part(a_low, b_high))


def dot(a, b):
    return product(a, b, ((1,), (0,)))


def tdot(a, b):
    return product(a, b, ((0,), (0,)))


def bdot(a, b):
    return jnp.dot(a, b, preferred_element_type=F32)


def call(kernel, outs, specs, flops, moved, scratch=(), limit=16, outs_at=None):
    return pl.pallas_call(
        kernel,
        out_shape=outs,
        in_specs=specs,
        out_specs=jax.tree.map(lambda _: VMEM, outs) if outs_at is None else outs_at,
        scratch_shapes=scratch,
        compiler_params=pltpu.CompilerParams(vmem_limit_bytes=limit * 2**20),
        cost_estimate=pl.CostEstimate(flops=flops, bytes_accessed=moved, transcendentals=0),
    )


def rows_of(ref, j, part):
    rows, parts, blocks, lanes = ref.shape
    flat = ref.reshape(rows * parts * blocks, lanes)
    return flat, pl.ds(part * blocks + j, rows, stride=parts * blocks)


def start_kernel(flags_ref, residual_hbm, *refs):
    given = (len(refs) - 5) // 2
    sources, loaded = refs[:given], refs[given : 2 * given]
    scaled_ref, keep_ref, send_ref, residual_ref, sems = refs[2 * given :]
    modes_ref, maps_ref = loaded[:2]
    copies = [
        pltpu.make_async_copy(source, target, sems.at[i])
        for i, (source, target) in enumerate(zip((residual_hbm,) + sources, (residual_ref,) + loaded))
    ]
    for copy in copies:
        copy.start()
    is_even, is_edge, is_upper = (flags_ref[i] > 0 for i in range(3))
    per, _, loads = scaled_ref.shape
    lanes = residual_ref.shape[-1]
    total = jnp.zeros((modes_ref.shape[1], loads), F32)
    copies[0].wait()
    copies[1].wait()
    for j in range(per):
        is_far = is_even if j == 0 else jnp.logical_not(is_even)
        scale = jnp.where(is_edge & is_far, 1.0, 0.5).astype(F32)
        for part in range(loads // lanes):
            flat, rows = rows_of(residual_ref, j, part)
            scaled_ref[j, :, part * lanes : (part + 1) * lanes] = (flat[rows, :] * scale).astype(BF)
        total += bdot(modes_ref[j], scaled_ref[j])
    copies[2].wait()
    mapped = tdot(maps_ref[0], total)
    for i, values in enumerate((total, mapped)):
        low, high = values[:, : loads // 2], values[:, loads // 2 :]
        keep_ref[i] = jnp.where(is_upper, high, low)
        send_ref[i] = jnp.where(is_upper, low, high)
    for copy in copies[3:]:
        copy.wait()


def local_kernel(flags_ref, scaled_ref, inverse_hbm, modes_ref, map_ref, near_ref, far_ref, near_modes, far_modes, far_out, mapped_out, inverse_ref, rows_ref, sem):
    copy = pltpu.make_async_copy(inverse_hbm, inverse_ref, sem)
    copy.start()
    loads = scaled_ref.shape[-1]
    is_even = flags_ref[0] > 0
    low_modes, high_modes = (modes_ref[j].T for j in range(2))
    near_modes[...] = jnp.where(is_even, high_modes, low_modes)
    far_modes[...] = jnp.where(is_even, low_modes, high_modes)
    far_out[loads:] = jnp.where(is_even, modes_ref[0], modes_ref[1])
    turned = map_ref[0].T
    high = turned.astype(BF)
    low = (turned - high.astype(F32)).astype(BF)
    near = jnp.where(is_even, modes_ref[1], modes_ref[0])
    mapped_out[...] = (bdot(high, near) + bdot(low, near)).astype(BF)
    copy.wait()
    rows, per, columns = inverse_ref.shape
    inverse = inverse_ref[...].reshape(rows * per, columns)
    lanes = rows_ref.shape[-1]
    products = [bdot(inverse, scaled_ref[j]) for j in range(per)]
    for part in range(loads // lanes):
        here = slice(part * lanes, (part + 1) * lanes)
        for j in range(per):
            rows_ref[j, part] = products[j][:, here]
        low, high = (rows_ref[j, part, pl.ds(j, rows, stride=per), :] for j in range(per))
        near, far = jnp.where(is_even, high, low), jnp.where(is_even, low, high)
        near_ref[:, here] = near
        far_ref[:, here] = far
        far_out[here] = far.astype(BF).T


def pair_kernel(keep_ref, got_ref, same_ref, cross_ref, map_ref, coarse_ref, pair_ref, own_ref, sent_ref, share_ref):
    coarse = keep_ref[0] + got_ref[0]
    for i in range(same_ref.shape[0]):
        coarse += same_ref[i].astype(F32)
    pair = tdot(map_ref[0], coarse)
    for i in range(cross_ref.shape[0]):
        pair += cross_ref[i].astype(F32)
    own = tdot(map_ref[1], pair)
    coarse_ref[...] = coarse
    pair_ref[...] = pair
    own_ref[...] = own
    sent_ref[...] = own.astype(BF)
    share_ref[...] = coarse.astype(BF)


def offer_kernel(coarse_ref, near_modes, mapped_ref, near_fix_ref, out_ref):
    loads = near_fix_ref.shape[-1]
    out_ref[:loads] = (near_fix_ref[...] + bdot(near_modes[...], coarse_ref[...])).astype(BF).T
    out_ref[loads:] = mapped_ref[...]


def turn_kernel(near_ref, far_ref, near_out, far_out):
    near_out[...] = near_ref[...].T
    for i in range(far_ref.shape[0]):
        far_out[i] = far_ref[i].T


def level_kernel(level, own_ref, got_ref, map_ref, value_ref, next_ref, sent_ref):
    value = own_ref[...] + got_ref[...].astype(F32)
    value_ref[...] = value
    following = tdot(map_ref[level], value)
    next_ref[...] = following
    sent_ref[...] = following.astype(BF)


def down_kernel(own_ref, got_ref, map_ref, root_ref, coarse_ref, *refs):
    values, fields_ref = refs[:-1], refs[-1]
    field = dot(root_ref[...], own_ref[...] + got_ref[...].astype(F32))
    for level in reversed(range(1, map_ref.shape[0])):
        field = dot(map_ref[level], field) + values[level - 1][...]
    fields_ref[0] = (dot(map_ref[0], field) + coarse_ref[...]).astype(BF)
    fields_ref[1] = field.astype(BF)


def near_kernel(fields_ref, near_modes, near_in_ref, near_fix_ref, near_out, near_bf):
    loads = near_fix_ref.shape[-1]
    own = near_fix_ref[...] + bdot(near_modes[...], fields_ref[0])
    other = near_in_ref[:, :loads].astype(F32) + bdot(near_in_ref[:, loads:], fields_ref[1])
    near = 0.5 * own + 0.5 * other
    near_out[...] = near
    near_bf[...] = near.astype(BF)


def far_kernel(flags_ref, fields_ref, near_ref, far_modes, far_in_ref, far_fix_ref, far_out, far_bf, mine_bf):
    loads = far_fix_ref.shape[-1]
    field = fields_ref[0]
    scale = jnp.where(flags_ref[1] > 0, 1.0, 0.5).astype(F32)
    far = (far_fix_ref[...] + bdot(far_modes[...], field)) * scale
    far_out[...] = far
    far_bf[...] = far.astype(BF)
    mine_bf[0] = far.astype(BF)
    mine_bf[1] = near_ref[...]
    for i in range(far_in_ref.shape[0]):
        block = far_in_ref[i, :, :loads].astype(F32) + bdot(far_in_ref[i, :, loads:], field)
        mine_bf[2 + i] = (block * scale).astype(BF)


def note_slots(slots_ref, first, end, number, list_ref):
    for i in range(list_ref.shape[1]):
        list_ref[0, i], list_ref[1, i] = 0, end - first

    def note(k, found):
        slot = slots_ref[k] - first
        is_here = (slot >= 0) & (slot < end - first)

        @pl.when(is_here)
        def _():
            list_ref[0, found], list_ref[1, found] = k, slot

        return found + is_here.astype(jnp.int32)

    list_ref[2, 0] = lax.fori_loop(0, number, note, 0)


def add_products(list_ref, matrix_ref, sources, values_ref, total):
    end = 0
    for source in sources:
        values_ref[end : end + source.shape[0]] = source[...]
        end += source.shape[0]
    values_ref[end] = jnp.zeros(values_ref.shape[1:], BF)
    found = list_ref[2, 0]
    most = 8

    def add(first, width):
        places = [first + i for i in range(width)]
        matrices = jnp.concatenate([matrix_ref[list_ref[0, at]] for at in places], axis=1)
        values = jnp.concatenate([values_ref[list_ref[1, at]] for at in places], axis=0)
        total[...] += bdot(matrices, values)

    def whole(step, carry):
        add(step * most, most)
        return carry

    steps = found // most
    lax.fori_loop(0, steps, whole, 0)
    left = found - steps * most
    for width in range(2, most + 1, 2):

        @pl.when((left > width - 2) & (left <= width))
        def _():
            add(steps * most, width)


def pick_kernel(flags_ref, inverse_ref, picked_ref):
    inverse = inverse_ref[...]
    picked_ref[...] = jnp.where(flags_ref[0] > 0, inverse[:, 0, :], inverse[:, 1, :])


def couple_kernel(late, slots_ref, flags_ref, matrix_ref, mine_ref, core_ref, total_ref, late_list_ref, values_ref, list_ref):
    @pl.when(flags_ref[1] > 0)
    def _():
        total_ref[...] = jnp.zeros(total_ref.shape, F32)
        sources = mine_ref, core_ref
        here = sum(source.shape[0] for source in sources)
        number = matrix_ref.shape[0]
        note_slots(slots_ref, 0, here, number, list_ref)
        note_slots(slots_ref, here, here + late, number, late_list_ref)
        add_products(list_ref, matrix_ref, sources, values_ref, total_ref)


def finish_kernel(list_ref, flags_ref, matrix_ref, picked_ref, total_ref, late_ref, late_core_ref, far_ref, far_in_ref, near_ref, out_ref, sum_ref, values_ref):
    is_even = flags_ref[0] > 0
    is_edge = flags_ref[1] > 0

    @pl.when(is_edge)
    def _():
        sum_ref[...] = total_ref[...]
        add_products(list_ref, matrix_ref, (late_ref, late_core_ref), values_ref, sum_ref)
        sum_ref[...] = far_ref[...] - bdot(picked_ref[...], sum_ref[...].astype(BF))

    @pl.when(jnp.logical_not(is_edge))
    def _():
        sum_ref[...] = far_ref[...] + far_in_ref[...].astype(F32)

    _, parts, _, lanes = out_ref.shape
    for part in range(parts):
        columns = slice(part * lanes, (part + 1) * lanes)
        far, near = sum_ref[:, columns], near_ref[:, columns]
        for j, values in enumerate((jnp.where(is_even, far, near), jnp.where(is_even, near, far))):
            flat, rows = rows_of(out_ref, j, part)
            flat[rows, :] = values


def after(x, *others):
    return lax.optimization_barrier((x,) + others)[0]


def shards(subs, blks, residual, stiffness, pattern, neumann_inv, dirichlet_inv, basis, node_ops, root_inv):
    here = lax.axis_index("sub")
    mine = lax.axis_index("blk")
    _, per, block, loads = residual.shape
    width = basis.shape[-1]
    coupled = pattern.shape[-1]
    levels = node_ops.shape[1]
    lanes = 128
    parts = loads // lanes
    assert per == 2 and levels > 2
    even = here % 2 == 0
    edge = (here == 0) | (here == subs - 1)
    upper = mine % 2 == 1
    flags = jnp.stack([even, edge, upper]).astype(jnp.int32)
    go = functools.partial(route, subs=subs, blks=blks)
    others = range(2, blks, 2)
    shape = jax.ShapeDtypeStruct
    half_shape = width, loads // 2
    small = 2 * width * width * loads // 2
    large = 10**11

    def swap(x, sub=0, blk=0):
        return go(x, target=lambda s, b: (s ^ sub, b ^ blk))

    def joined(x):
        other = swap(x, blk=1)
        return jnp.concatenate([jnp.where(upper, other, x), jnp.where(upper, x, other)], axis=-1)

    def turned(x):
        return jnp.transpose(x[0], (1, 0, 2))

    modes = jnp.transpose(basis[0], (0, 2, 1))
    laid = jnp.transpose(residual[0].reshape(per, block, parts, lanes), (1, 2, 0, 3))

    given = modes, node_ops[0]
    modes, maps, scaled, keep, sent = call(
        start_kernel,
        tuple(shape(x.shape, x.dtype) for x in given)
        + (shape((per, block, loads), BF),)
        + (shape((2,) + half_shape, F32),) * 2,
        [SMEM] + [HBM] * (1 + len(given)),
        2 * per * block * width * loads,
        0,
        [pltpu.VMEM(laid.shape, F32), pltpu.SemaphoreType.DMA((1 + len(given),))],
        52,
    )(flags, laid, *given)
    got = swap(sent, blk=1)
    neumann = turned(neumann_inv)
    near_fix, far_fix, near_modes, far_modes, to_far, mapped_modes = call(
        local_kernel,
        (shape((block, loads), F32),) * 2
        + (shape((block, width), BF),) * 2
        + (shape((loads + width, block), BF), shape((width, block), BF)),
        [SMEM, VMEM, HBM, VMEM, VMEM],
        large,
        0,
        [
            pltpu.VMEM(neumann.shape, BF),
            pltpu.VMEM((per, parts, per * block, lanes), F32),
            pltpu.SemaphoreType.DMA(()),
        ],
        16,
    )(flags, after(scaled, got), neumann, modes, maps)
    half_bf, mapped_bf = (keep[0] + got[0]).astype(BF), (keep[1] + got[1]).astype(BF)

    same = jnp.stack([swap(half_bf, blk=d) for d in others])
    cross = jnp.stack([swap(mapped_bf, sub=1, blk=d) for d in (0,) + tuple(others)])
    cross, near_fix, to_far = lax.optimization_barrier((cross, near_fix, to_far))
    coarse, value, own, own_bf, share = call(
        pair_kernel,
        (shape(half_shape, F32),) * 3
        + (shape(half_shape, BF),) * 2,
        [VMEM] * 5,
        3 * small,
        8 * width * width,
        limit=4,
    )(keep, got, same, cross, maps)
    offer = call(
        offer_kernel,
        shape(to_far.shape, BF),
        [VMEM] * 4,
        3 * 10**9,
        0,
    )(joined(share), near_modes, mapped_modes, near_fix)
    from_sibling = swap(offer, sub=1)
    from_others = jnp.stack([swap(to_far, blk=d) for d in others])
    values = [value]
    for level in range(2, levels):
        value, own, own_bf = call(
            functools.partial(level_kernel, level),
            (shape(half_shape, F32),) * 2 + (shape(half_shape, BF),),
            [VMEM] * 3,
            2*10**9,
            4 * width * width,
            limit=4,
        )(own, swap(own_bf, sub=2 ** (level - 1)), maps)
        values.append(value)
    fields = call(
        down_kernel,
        shape((2,) + half_shape, BF),
        [VMEM] * (5 + len(values)),
        (levels + 3) * small,
        4 * (levels + 2) * width * width,
        limit=4,
    )(own, swap(own_bf, sub=subs // 2), maps, root_inv, coarse, *values)
    far_id = jnp.where(even, 0, per - 1)
    matrix = lax.dynamic_index_in_dim(stiffness[0], after(far_id, own_bf), 0, False)
    fields, from_sibling, from_others, matrix = lax.optimization_barrier(
        (fields, from_sibling, from_others, matrix)
    )
    from_sibling, from_others = call(
        turn_kernel,
        (shape((block, loads + width), BF), shape((len(others), block, loads + width), BF)),
        [VMEM] * 2,
        10**9,
        0,
    )(from_sibling, from_others)
    fields, from_sibling, from_others = lax.optimization_barrier((joined(fields), from_sibling, from_others))

    count = 2 + len(others)
    face = 2 * block * width * loads
    near, near_bf = call(
        near_kernel,
        (shape((block, loads), F32), shape((block, loads), BF)),
        [VMEM] * 4,
        2 * face,
        block * loads * 8,
    )(fields, near_modes, from_sibling, near_fix)
    late = jnp.stack(
        [
            go(near_bf, target=lambda s, b, d=d: (s, b ^ d) if s in (0, subs - 1) else (s, b ^ 1))
            for d in others
        ]
    )
    far, far_bf, mine_bf = call(
        far_kernel,
        (shape((block, loads), F32), shape((block, loads), BF), shape((count, block, loads), BF)),
        [SMEM] + [VMEM] * 5,
        10**11,
        count * block * loads * 8,
    )(flags, fields, near_bf, far_modes, from_others, far_fix)

    core = swap(mine_bf, blk=1)
    picked = call(
        pick_kernel,
        shape((block, block), BF),
        [SMEM, VMEM],
        1000,
        0,
    )(after(flags, near_bf), turned(dirichlet_inv))
    far_in = go(
        far_bf,
        target=lambda s, b: (s, b ^ 1) if s in (0, subs - 1) else (s - 1 if s % 2 == 0 else s + 1, b),
    )
    columns = pattern[0, far_id]
    offset = (columns // per) ^ mine
    is_near = columns % per != far_id
    distant = offset // 2
    slots = jnp.where(
        is_near & (distant > 0),
        2 * count + (offset % 2) * len(others) + distant - 1,
        (offset % 2) * count + jnp.where(is_near, 1, jnp.where(distant > 0, 1 + distant, 0)),
    )
    first = 2 * count
    more = 2 * len(others)
    listed = (3, -(-coupled // 8) * 8)
    total, late_list = call(
        functools.partial(couple_kernel, more),
        (shape((block, loads), F32), shape(listed, jnp.int32)),
        [SMEM, SMEM] + [VMEM] * 3,
        1000,
        2 * coupled * block * block,
        [pltpu.VMEM((first + 1, block, loads), BF), pltpu.SMEM(listed, jnp.int32)],
        outs_at=(VMEM, SMEM),
    )(slots, flags, matrix, mine_bf, core)
    late, total, picked = lax.optimization_barrier((late, total, picked))
    late_core = swap(late, blk=1)
    result = call(
        finish_kernel,
        shape((block, parts, per, lanes), F32),
        [SMEM, SMEM] + [VMEM] * 8,
        2 * block * block * loads,
        block * loads * 16,
        [
            pltpu.VMEM((block, loads), F32),
            pltpu.VMEM((more + 1, block, loads), BF),
        ],
    )(late_list, flags, matrix, picked, total, late, late_core, far, far_in, near)
    return jnp.transpose(result, (2, 0, 1, 3)).reshape(per, block, loads)[None]


def solution(mesh):
    placed = (
        P("sub", "blk", None, None),
        P("sub", "blk", None, None, None),
        P("sub", "blk", None),
        P("sub", "blk", None, None),
        P("sub", "blk", None, None),
        P("sub", "blk", None, None),
        P("sub", None, None, None),
        P(),
    )
    return jax.shard_map(
        functools.partial(shards, mesh.shape["sub"], mesh.shape["blk"]),
        mesh=mesh,
        in_specs=placed,
        out_specs=P("sub", "blk", None, None),
        check_vma=False,
    )
```

```python
import functools

import jax
import jax.numpy as jnp
from jax import lax
from jax.experimental import pallas as pl
from jax.experimental.pallas import tpu as pltpu
from jax.sharding import PartitionSpec as P

BF = jnp.bfloat16
F32 = jnp.float32
VMEM = pl.BlockSpec(memory_space=pltpu.VMEM)
SMEM = pl.BlockSpec(memory_space=pltpu.SMEM)
HBM = pl.BlockSpec(memory_space=pltpu.HBM)


def route(x, subs, blks, target):
    pairs = []
    for s in range(subs):
        for b in range(blks):
            to = target(s, b)
            if to is not None and 0 <= to[0] < subs:
                pairs.append((s * blks + b, to[0] * blks + to[1]))
    return lax.ppermute(x, ("sub", "blk"), pairs)


def product(a, b, dims):
    a_high, b_high = a.astype(BF), b.astype(BF)
    a_low, b_low = (a - a_high.astype(F32)).astype(BF), (b - b_high.astype(F32)).astype(BF)
    part = functools.partial(
        lax.dot_general, dimension_numbers=(dims, ((), ())), preferred_element_type=F32
    )
    return part(a_high, b_high) + (part(a_high, b_low) + part(a_low, b_high))


def dot(a, b):
    return product(a, b, ((1,), (0,)))


def tdot(a, b):
    return product(a, b, ((0,), (0,)))


def bdot(a, b):
    return jnp.dot(a, b, preferred_element_type=F32)


def call(kernel, outs, specs, flops, moved, scratch=(), limit=16, outs_at=None):
    return pl.pallas_call(
        kernel,
        out_shape=outs,
        in_specs=specs,
        out_specs=jax.tree.map(lambda _: VMEM, outs) if outs_at is None else outs_at,
        scratch_shapes=scratch,
        compiler_params=pltpu.CompilerParams(vmem_limit_bytes=limit * 2**20),
        cost_estimate=pl.CostEstimate(flops=flops, bytes_accessed=moved, transcendentals=0),
    )


def position():
    here, last = lax.axis_index("sub"), lax.axis_size("sub") - 1
    return lax.rem(here, 2) == 0, (here == 0) | (here == last), lax.rem(lax.axis_index("blk"), 2) == 1


def rows_of(ref, j, part):
    rows, parts, blocks, lanes = ref.shape
    flat = ref.reshape(rows * parts * blocks, lanes)
    return flat, pl.ds(part * blocks + j, rows, stride=parts * blocks)


def start_kernel(residual_hbm, *refs):
    given = (len(refs) - 5) // 2
    sources, loaded = refs[:given], refs[given : 2 * given]
    scaled_ref, keep_ref, send_ref, residual_ref, sems = refs[2 * given :]
    modes_ref, maps_ref = loaded[:2]
    copies = [
        pltpu.make_async_copy(source, target, sems.at[i])
        for i, (source, target) in enumerate(zip((residual_hbm,) + sources, (residual_ref,) + loaded))
    ]
    for copy in copies:
        copy.start()
    is_even, is_edge, is_upper = position()
    per, _, loads = scaled_ref.shape
    lanes = residual_ref.shape[-1]
    total = jnp.zeros((modes_ref.shape[1], loads), F32)
    copies[0].wait()
    copies[1].wait()
    for j in range(per):
        is_far = is_even if j == 0 else jnp.logical_not(is_even)
        scale = jnp.where(is_edge & is_far, 1.0, 0.5).astype(F32)
        for part in range(loads // lanes):
            flat, rows = rows_of(residual_ref, j, part)
            scaled_ref[j, :, part * lanes : (part + 1) * lanes] = (flat[rows, :] * scale).astype(BF)
        total += bdot(modes_ref[j], scaled_ref[j])
    copies[2].wait()
    mapped = tdot(maps_ref[0], total)
    for i, values in enumerate((total, mapped)):
        low, high = values[:, : loads // 2], values[:, loads // 2 :]
        keep_ref[i] = jnp.where(is_upper, high, low)
        send_ref[i] = jnp.where(is_upper, low, high)
    for copy in copies[3:]:
        copy.wait()


def local_kernel(flags_ref, scaled_ref, inverse_hbm, modes_ref, map_ref, near_ref, far_ref, near_modes, far_modes, far_out, mapped_out, inverse_ref, rows_ref, sem):
    copy = pltpu.make_async_copy(inverse_hbm, inverse_ref, sem)
    copy.start()
    loads = scaled_ref.shape[-1]
    is_even = flags_ref[0] > 0
    low_modes, high_modes = (modes_ref[j].T for j in range(2))
    near_modes[...] = jnp.where(is_even, high_modes, low_modes)
    far_modes[...] = jnp.where(is_even, low_modes, high_modes)
    far_out[loads:] = jnp.where(is_even, modes_ref[0], modes_ref[1])
    turned = map_ref[0].T
    high = turned.astype(BF)
    low = (turned - high.astype(F32)).astype(BF)
    near = jnp.where(is_even, modes_ref[1], modes_ref[0])
    mapped_out[...] = (bdot(high, near) + bdot(low, near)).astype(BF)
    copy.wait()
    rows, per, columns = inverse_ref.shape
    inverse = inverse_ref[...].reshape(rows * per, columns)
    lanes = rows_ref.shape[-1]
    products = [bdot(inverse, scaled_ref[j]) for j in range(per)]
    for part in range(loads // lanes):
        here = slice(part * lanes, (part + 1) * lanes)
        for j in range(per):
            rows_ref[j, part] = products[j][:, here]
        low, high = (rows_ref[j, part, pl.ds(j, rows, stride=per), :] for j in range(per))
        near, far = jnp.where(is_even, high, low), jnp.where(is_even, low, high)
        near_ref[:, here] = near
        far_ref[:, here] = far
        far_out[here] = far.astype(BF).T


def pair_kernel(keep_ref, got_ref, same_ref, cross_ref, map_ref, coarse_ref, pair_ref, own_ref, sent_ref, share_ref):
    coarse = keep_ref[0] + got_ref[0]
    for i in range(same_ref.shape[0]):
        coarse += same_ref[i].astype(F32)
    pair = tdot(map_ref[0], coarse)
    for i in range(cross_ref.shape[0]):
        pair += cross_ref[i].astype(F32)
    own = tdot(map_ref[1], pair)
    coarse_ref[...] = coarse
    pair_ref[...] = pair
    own_ref[...] = own
    sent_ref[...] = own.astype(BF)
    share_ref[...] = coarse.astype(BF)


def offer_kernel(coarse_ref, near_modes, mapped_ref, near_fix_ref, out_ref):
    loads = near_fix_ref.shape[-1]
    out_ref[:loads] = (near_fix_ref[...] + bdot(near_modes[...], coarse_ref[...])).astype(BF).T
    out_ref[loads:] = mapped_ref[...]


def turn_kernel(near_ref, far_ref, near_out, far_out):
    near_out[...] = near_ref[...].T
    for i in range(far_ref.shape[0]):
        far_out[i] = far_ref[i].T


def level_kernel(level, own_ref, got_ref, map_ref, value_ref, next_ref, sent_ref):
    value = own_ref[...] + got_ref[...].astype(F32)
    value_ref[...] = value
    following = tdot(map_ref[level], value)
    next_ref[...] = following
    sent_ref[...] = following.astype(BF)


def down_kernel(own_ref, got_ref, map_ref, root_ref, coarse_ref, *refs):
    values, fields_ref = refs[:-1], refs[-1]
    field = dot(root_ref[...], own_ref[...] + got_ref[...].astype(F32))
    for level in reversed(range(1, map_ref.shape[0])):
        field = dot(map_ref[level], field) + values[level - 1][...]
    fields_ref[0] = (dot(map_ref[0], field) + coarse_ref[...]).astype(BF)
    fields_ref[1] = field.astype(BF)


def near_kernel(fields_ref, near_modes, near_in_ref, near_fix_ref, near_out, near_bf):
    loads = near_fix_ref.shape[-1]
    own = near_fix_ref[...] + bdot(near_modes[...], fields_ref[0])
    other = near_in_ref[:, :loads].astype(F32) + bdot(near_in_ref[:, loads:], fields_ref[1])
    near = 0.5 * own + 0.5 * other
    near_out[...] = near
    near_bf[...] = near.astype(BF)


def far_kernel(fields_ref, near_ref, far_modes, far_in_ref, far_fix_ref, far_out, far_bf, mine_bf):
    loads = far_fix_ref.shape[-1]
    field = fields_ref[0]
    scale = jnp.where(position()[1], 1.0, 0.5).astype(F32)
    far = (far_fix_ref[...] + bdot(far_modes[...], field)) * scale
    far_out[...] = far
    far_bf[...] = far.astype(BF)
    mine_bf[0] = far.astype(BF)
    mine_bf[1] = near_ref[...]
    for i in range(far_in_ref.shape[0]):
        block = far_in_ref[i, :, :loads].astype(F32) + bdot(far_in_ref[i, :, loads:], field)
        mine_bf[2 + i] = (block * scale).astype(BF)


def note_slots(slots_ref, first, end, number, list_ref):
    for i in range(list_ref.shape[1]):
        list_ref[0, i], list_ref[1, i] = 0, end - first

    def note(k, found):
        slot = slots_ref[k] - first
        is_here = (slot >= 0) & (slot < end - first)

        @pl.when(is_here)
        def _():
            list_ref[0, found], list_ref[1, found] = k, slot

        return found + is_here.astype(jnp.int32)

    list_ref[2, 0] = lax.fori_loop(0, number, note, 0)


def add_products(list_ref, matrix_ref, sources, values_ref, total):
    end = 0
    for source in sources:
        values_ref[end : end + source.shape[0]] = source[...]
        end += source.shape[0]
    values_ref[end] = jnp.zeros(values_ref.shape[1:], BF)
    found = list_ref[2, 0]
    most = 8

    def add(first, width):
        places = [first + i for i in range(width)]
        matrices = jnp.concatenate([matrix_ref[list_ref[0, at]] for at in places], axis=1)
        values = jnp.concatenate([values_ref[list_ref[1, at]] for at in places], axis=0)
        total[...] += bdot(matrices, values)

    def whole(step, carry):
        add(step * most, most)
        return carry

    steps = found // most
    lax.fori_loop(0, steps, whole, 0)
    left = found - steps * most
    for width in range(2, most + 1, 2):

        @pl.when((left > width - 2) & (left <= width))
        def _():
            add(steps * most, width)


def pick_kernel(flags_ref, inverse_ref, picked_ref):
    inverse = inverse_ref[...]
    picked_ref[...] = jnp.where(flags_ref[0] > 0, inverse[:, 0, :], inverse[:, 1, :])


def couple_kernel(late, slots_ref, flags_ref, matrix_ref, mine_ref, core_ref, total_ref, late_list_ref, values_ref, list_ref):
    @pl.when(flags_ref[1] > 0)
    def _():
        total_ref[...] = jnp.zeros(total_ref.shape, F32)
        sources = mine_ref, core_ref
        here = sum(source.shape[0] for source in sources)
        number = matrix_ref.shape[0]
        note_slots(slots_ref, 0, here, number, list_ref)
        note_slots(slots_ref, here, here + late, number, late_list_ref)
        add_products(list_ref, matrix_ref, sources, values_ref, total_ref)


def finish_kernel(list_ref, matrix_ref, picked_ref, total_ref, late_ref, late_core_ref, far_ref, far_in_ref, near_ref, out_ref, sum_ref, values_ref):
    is_even, is_edge, _ = position()

    @pl.when(is_edge)
    def _():
        sum_ref[...] = total_ref[...]
        add_products(list_ref, matrix_ref, (late_ref, late_core_ref), values_ref, sum_ref)
        sum_ref[...] = far_ref[...] - bdot(picked_ref[...], sum_ref[...].astype(BF))

    @pl.when(jnp.logical_not(is_edge))
    def _():
        sum_ref[...] = far_ref[...] + far_in_ref[...].astype(F32)

    _, parts, _, lanes = out_ref.shape
    for part in range(parts):
        columns = slice(part * lanes, (part + 1) * lanes)
        far, near = sum_ref[:, columns], near_ref[:, columns]
        for j, values in enumerate((jnp.where(is_even, far, near), jnp.where(is_even, near, far))):
            flat, rows = rows_of(out_ref, j, part)
            flat[rows, :] = values


def after(x, *others):
    return lax.optimization_barrier((x,) + others)[0]


def shards(subs, blks, residual, stiffness, pattern, neumann_inv, dirichlet_inv, basis, node_ops, root_inv):
    here = lax.axis_index("sub")
    mine = lax.axis_index("blk")
    _, per, block, loads = residual.shape
    width = basis.shape[-1]
    coupled = pattern.shape[-1]
    levels = node_ops.shape[1]
    lanes = 128
    parts = loads // lanes
    assert per == 2 and levels > 2
    even = here % 2 == 0
    edge = (here == 0) | (here == subs - 1)
    upper = mine % 2 == 1
    flags = jnp.stack([even, edge, upper]).astype(jnp.int32)
    go = functools.partial(route, subs=subs, blks=blks)
    others = range(2, blks, 2)
    shape = jax.ShapeDtypeStruct
    half_shape = width, loads // 2
    small = 2 * width * width * loads // 2
    large = 10**11

    def swap(x, sub=0, blk=0):
        return go(x, target=lambda s, b: (s ^ sub, b ^ blk))

    def joined(x):
        other = swap(x, blk=1)
        return jnp.concatenate([jnp.where(upper, other, x), jnp.where(upper, x, other)], axis=-1)

    def turned(x):
        return jnp.transpose(x[0], (1, 0, 2))

    modes = jnp.transpose(basis[0], (0, 2, 1))
    laid = jnp.transpose(residual[0].reshape(per, block, parts, lanes), (1, 2, 0, 3))

    given = modes, node_ops[0]
    modes, maps, scaled, keep, sent = call(
        start_kernel,
        tuple(shape(x.shape, x.dtype) for x in given)
        + (shape((per, block, loads), BF),)
        + (shape((2,) + half_shape, F32),) * 2,
        [HBM] * (1 + len(given)),
        2 * per * block * width * loads,
        0,
        [pltpu.VMEM(laid.shape, F32), pltpu.SemaphoreType.DMA((1 + len(given),))],
        52,
    )(laid, *given)
    got = swap(sent, blk=1)
    neumann = turned(neumann_inv)
    near_fix, far_fix, near_modes, far_modes, to_far, mapped_modes = call(
        local_kernel,
        (shape((block, loads), F32),) * 2
        + (shape((block, width), BF),) * 2
        + (shape((loads + width, block), BF), shape((width, block), BF)),
        [SMEM, VMEM, HBM, VMEM, VMEM],
        large,
        0,
        [
            pltpu.VMEM(neumann.shape, BF),
            pltpu.VMEM((per, parts, per * block, lanes), F32),
            pltpu.SemaphoreType.DMA(()),
        ],
        16,
    )(flags, after(scaled, got), neumann, modes, maps)
    half_bf, mapped_bf = (keep[0] + got[0]).astype(BF), (keep[1] + got[1]).astype(BF)

    same = jnp.stack([swap(half_bf, blk=d) for d in others])
    cross = jnp.stack([swap(mapped_bf, sub=1, blk=d) for d in (0,) + tuple(others)])
    cross, near_fix, to_far = lax.optimization_barrier((cross, near_fix, to_far))
    coarse, value, own, own_bf, share = call(
        pair_kernel,
        (shape(half_shape, F32),) * 3
        + (shape(half_shape, BF),) * 2,
        [VMEM] * 5,
        3 * small,
        8 * width * width,
        limit=4,
    )(keep, got, same, cross, maps)
    offer = call(
        offer_kernel,
        shape(to_far.shape, BF),
        [VMEM] * 4,
        3 * 10**9,
        0,
    )(joined(share), near_modes, mapped_modes, near_fix)
    from_sibling = swap(offer, sub=1)
    from_others = jnp.stack([swap(to_far, blk=d) for d in others])
    values = [value]
    for level in range(2, levels):
        value, own, own_bf = call(
            functools.partial(level_kernel, level),
            (shape(half_shape, F32),) * 2 + (shape(half_shape, BF),),
            [VMEM] * 3,
            2*10**9,
            4 * width * width,
            limit=4,
        )(own, swap(own_bf, sub=2 ** (level - 1)), maps)
        values.append(value)
    fields = call(
        down_kernel,
        shape((2,) + half_shape, BF),
        [VMEM] * (5 + len(values)),
        (levels + 3) * small,
        4 * (levels + 2) * width * width,
        limit=4,
    )(own, swap(own_bf, sub=subs // 2), maps, root_inv, coarse, *values)
    far_id = jnp.where(even, 0, per - 1)
    matrix = lax.dynamic_index_in_dim(stiffness[0], after(far_id, own_bf), 0, False)
    fields, from_sibling, from_others, matrix = lax.optimization_barrier(
        (fields, from_sibling, from_others, matrix)
    )
    from_sibling, from_others = call(
        turn_kernel,
        (shape((block, loads + width), BF), shape((len(others), block, loads + width), BF)),
        [VMEM] * 2,
        10**9,
        0,
    )(from_sibling, from_others)
    fields, from_sibling, from_others = lax.optimization_barrier((joined(fields), from_sibling, from_others))

    count = 2 + len(others)
    face = 2 * block * width * loads
    near, near_bf = call(
        near_kernel,
        (shape((block, loads), F32), shape((block, loads), BF)),
        [VMEM] * 4,
        2 * face,
        block * loads * 8,
    )(fields, near_modes, from_sibling, near_fix)
    late = jnp.stack(
        [
            go(near_bf, target=lambda s, b, d=d: (s, b ^ d) if s in (0, subs - 1) else (s, b ^ 1))
            for d in others
        ]
    )
    far, far_bf, mine_bf = call(
        far_kernel,
        (shape((block, loads), F32), shape((block, loads), BF), shape((count, block, loads), BF)),
        [VMEM] * 5,
        10**11,
        count * block * loads * 8,
    )(fields, near_bf, far_modes, from_others, far_fix)

    core = swap(mine_bf, blk=1)
    picked = call(
        pick_kernel,
        shape((block, block), BF),
        [SMEM, VMEM],
        1000,
        0,
    )(after(flags, near_bf), turned(dirichlet_inv))
    far_in = go(
        far_bf,
        target=lambda s, b: (s, b ^ 1) if s in (0, subs - 1) else (s - 1 if s % 2 == 0 else s + 1, b),
    )
    columns = pattern[0, far_id]
    offset = (columns // per) ^ mine
    is_near = columns % per != far_id
    distant = offset // 2
    slots = jnp.where(
        is_near & (distant > 0),
        2 * count + (offset % 2) * len(others) + distant - 1,
        (offset % 2) * count + jnp.where(is_near, 1, jnp.where(distant > 0, 1 + distant, 0)),
    )
    first = 2 * count
    more = 2 * len(others)
    listed = (3, -(-coupled // 8) * 8)
    total, late_list = call(
        functools.partial(couple_kernel, more),
        (shape((block, loads), F32), shape(listed, jnp.int32)),
        [SMEM, SMEM] + [VMEM] * 3,
        1000,
        2 * coupled * block * block,
        [pltpu.VMEM((first + 1, block, loads), BF), pltpu.SMEM(listed, jnp.int32)],
        outs_at=(VMEM, SMEM),
    )(slots, flags, matrix, mine_bf, core)
    late, total, picked = lax.optimization_barrier((late, total, picked))
    late_core = swap(late, blk=1)
    result = call(
        finish_kernel,
        shape((block, parts, per, lanes), F32),
        [SMEM] + [VMEM] * 8,
        2 * block * block * loads,
        block * loads * 16,
        [
            pltpu.VMEM((block, loads), F32),
            pltpu.VMEM((more + 1, block, loads), BF),
        ],
    )(late_list, matrix, picked, total, late, late_core, far, far_in, near)
    return jnp.transpose(result, (2, 0, 1, 3)).reshape(per, block, loads)[None]


def solution(mesh):
    placed = (
        P("sub", "blk", None, None),
        P("sub", "blk", None, None, None),
        P("sub", "blk", None),
        P("sub", "blk", None, None),
        P("sub", "blk", None, None),
        P("sub", "blk", None, None),
        P("sub", None, None, None),
        P(),
    )
    return jax.shard_map(
        functools.partial(shards, mesh.shape["sub"], mesh.shape["blk"]),
        mesh=mesh,
        in_specs=placed,
        out_specs=P("sub", "blk", None, None),
        check_vma=False,
    )
```
